256 devices in a mesh: row: 16 (over z_hi, x), col: 16 (over z_lo, y, core).
Axes of the slice: x: 4, y: 4, z: 8 (z_hi: 4, z_lo: 2; z = z_hi * 2 + z_lo), core: 2. Of those that a mesh axis runs over, the one named last changes fastest.
Arguments:
- hessian: float32 [16, 768, 16, 768], P('row', None, 'col'), may hold values from -6 to 6
- panels: float32 [16, 16, 48, 1024], P('row', 'col'), may hold values from -0.078125 to 0.078125
- factors: float32 [2, 512, 512], replicated, may hold values from -1.6 to 1.6, as said below
Outputs:
- updated: float32 [16, 768, 16, 768], P('row', None, 'col')
The draws below stay inside these ranges and needn't reach their ends.
Inputs may be any that keep to these rules, and one draw needn't show every extreme that they name: Each of the two factors is upper triangular, with diagonal entries from 0.8 to 1.6.
All inputs are finite; a program needn't handle non-finite values.
Results may differ from the reference program's by a relative error of at most 0.0001.
Values sent between devices are 32-bit elements; how exact they have to be, the bound alone decides.
A program may use at most 128 MiB of HBM per device.

```python
import math
import jax
import jax.numpy as jnp
from jax import lax

M = 12288
B = 512
W = 48
N_ROW = 16
N_COL = 16


def draw_factors(key, part):
    key = jax.random.fold_in(key, 7)
    upper_key, diag_key = jax.random.split(key)
    spread = jnp.clip(jax.random.normal(upper_key, (2, B, B), jnp.float32), -4.0, 4.0)
    diagonal_values = jax.random.uniform(diag_key, (2, B), jnp.float32, 0.8, 1.6)
    positions = jnp.arange(B)
    above = (positions[:, None] < positions[None, :]).astype(jnp.float32)
    identity_mask = (positions[:, None] == positions[None, :]).astype(jnp.float32)
    return spread * (0.5 / math.sqrt(B)) * above[None] + diagonal_values[:, :, None] * identity_mask[None]


def block_levels(key, shape, cuts, least, top_value):
    level, own = 1.0, jax.random.fold_in(key, 6)
    for position, shards_of in cuts:
        draws = jnp.exp(jax.random.uniform(jax.random.fold_in(own, position), (shards_of,), jnp.float32, least / len(cuts), top_value / len(cuts)))
        level = level * jnp.repeat(draws, shape[position] // shards_of).reshape([-1 if axis == position else 1 for axis in range(len(shape))])
    return level


def bell_draw(own_key, extent, scale, most, cuts=(), kind=jnp.bfloat16):
    values = scale * jax.random.normal(own_key, extent, jnp.float32)
    if cuts:
        values = values * block_levels(own_key, extent, cuts, -0.22, 0.18)
    return jnp.clip(values, -most, most).astype(kind)


def setup_inputs(seed: int = 0) -> dict:
    key_of = jax.random.split(jax.random.key(seed), 4)
    return {
        "hessian": bell_draw(key_of[0], (N_ROW, N_COL * W, N_COL, N_ROW * W), 1.0, 6.0, ((0, 16), (2, 16)), jnp.float32),
        "panels": bell_draw(key_of[1], (N_ROW, N_COL, W, 2 * B), (M // 2) ** -0.5, 0.078125, ((0, 16), (1, 16)), jnp.float32),
        "factors": draw_factors(jax.random.fold_in(key_of[3], 71), 0),
    }


PRECISE = lax.Precision.HIGHEST


def product(left_side, right_side):
    return jnp.dot(left_side, right_side, precision=PRECISE, preferred_element_type=jnp.float32)


def reference(hessian, panels, factors):
    full_matrix = hessian.reshape(N_ROW, N_COL, W, N_COL, N_ROW, W).transpose(0, 1, 2, 4, 3, 5).reshape(M, M)
    symmetric = 0.5 * (full_matrix + full_matrix.T)
    basis = panels.reshape(M, 2 * B)
    current = symmetric
    wy_pieces = []
    for panel_index in range(2):
        panel_basis = basis[:, panel_index * B:(panel_index + 1) * B]
        panel_factor = factors[panel_index]
        image = product(current, panel_basis)
        gram = product(panel_basis.T, image)
        middle = product(panel_factor.T, product(gram, panel_factor))
        wy_piece = product(image, panel_factor) - 0.5 * product(panel_basis, middle)
        wy_pieces.append(wy_piece)
        if panel_index == 0:
            current = symmetric - product(panel_basis, wy_piece.T) - product(wy_piece, panel_basis.T)
    wy_all = jnp.concatenate(wy_pieces, axis=1)
    updated = symmetric - product(basis, wy_all.T) - product(wy_all, basis.T)
    return updated.reshape(N_ROW, N_COL, W, N_ROW, N_COL, W).transpose(0, 1, 2, 4, 3, 5).reshape(N_ROW, N_COL * W, N_COL, N_ROW * W)
```

```python
import functools

import jax
import jax.numpy as jnp
from jax import lax
from jax.experimental import pallas as pl
from jax.experimental.pallas import tpu as pltpu
from jax.sharding import PartitionSpec as P

MESH = pl.DeviceIdType.MESH
F32, BF16 = jnp.float32, jnp.bfloat16
NX, NY, NZ = 4, 4, 8
W = 48
M = 768
B = 512
U = 2 * B


def split(value):
    high = value.astype(BF16)
    return high, (value - high.astype(F32)).astype(BF16)


def put(ref, where, value):
    high, low = split(value)
    ref[(0,) + where] = high
    ref[(1,) + where] = low


def mm(left, right, dims=((1,), (0,))):
    def one(a, b):
        return lax.dot_general(a, b, (dims, ((), ())), preferred_element_type=F32)

    return one(left[0], right[0]) + (one(left[0], right[1]) + one(left[1], right[0]))


NT = ((1,), (1,))


def hl(ref, *where):
    return ref[(0,) + where], ref[(1,) + where]


class Place:
    def __init__(self):
        row, col = lax.axis_index("row"), lax.axis_index("col")
        self.zh, self.x = row // NX, row % NX
        self.zl, self.y, self.k = col // (2 * NY), (col // 2) % NY, col % 2
        self.z = self.zh * 2 + self.zl
        self.f = row
        self.slot = self.slot_of(self.k, self.zl, self.y)

    def slot_of(self, k, zl, y):
        return k * 8 + zl * 4 + y

    def at(self, dx=0, dy=0, dz=0, dk=0):
        x, y, z = (self.x + dx) % NX, (self.y + dy) % NY, (self.z + dz) % NZ
        k = (self.k + dk) % 2
        return {"row": (z // 2) * NX + x, "col": (z % 2) * 2 * NY + y * 2 + k}

    def zl_peer(self):
        return {"col": (1 - self.zl) * 2 * NY + self.y * 2 + self.k, "row": self.f}


class Mail:
    def __init__(self, send_sems, recv_sems):
        self.send_sems, self.recv_sems, self.sent = send_sems, recv_sems, []

    def send(self, src, dst, target):
        index = len(self.sent)
        copy = pltpu.make_async_remote_copy(
            src, dst, self.send_sems.at[index], self.recv_sems.at[index], device_id=target, device_id_type=MESH
        )
        copy.start()
        self.sent.append(copy)
        return copy

    def close(self):
        for copy in self.sent:
            copy.wait_send()


def greet(partners):
    barrier = pltpu.get_barrier_semaphore()
    for target in partners:
        pl.semaphore_signal(barrier, inc=1, device_id=target, device_id_type=MESH)
    pl.semaphore_wait(barrier, len(partners))


def rows48(slot):
    return pl.ds(pl.multiple_of(slot * W, 8), W)


def gather_row(mail, here, buf):
    def block(zh, x):
        return buf.at[rows48(zh * NX + x)]

    mine = block(here.zh, here.x)
    far = [mail.send(mine, mine, here.at(dz=2 * d)) for d in (1, 2, 3)]
    last = [mail.send(mine, mine, here.at(dx=d)) for d in (1, 2, 3)]
    yield
    for d in (1, 2, 3):
        far[d - 1].wait_recv()
        got = block((here.zh + 4 - d) % 4, here.x)
        last += [mail.send(got, got, here.at(dx=e)) for e in (1, 2, 3)]
        yield
    for copy in last:
        copy.wait_recv()
    yield


def gather_col(mail, here, buf):
    def block(zl):
        return buf.at[rows48(here.slot_of(here.k, zl, here.y))]

    mine = block(here.zl)
    pair = mail.send(mine, mine, here.zl_peer())
    first = [mail.send(mine, mine, here.at(dy=d)) for d in (1, 2, 3)]
    yield
    pair.wait_recv()
    got = block(1 - here.zl)
    second = [mail.send(got, got, here.at(dy=d)) for d in (1, 2, 3)]
    yield
    last = []
    for zl, copies in ((here.zl, first), (1 - here.zl, second)):
        for copy in copies:
            copy.wait_recv()
        part = buf.at[pl.ds(pl.multiple_of((here.k * 8 + zl * 4) * W, 8), 4 * W)]
        last.append(mail.send(part, part, here.at(dk=1)))
        yield
    for copy in last:
        copy.wait_recv()
    yield


def all_reduce(mail, here, part, out, from_k, from_x, from_y, from_z):
    q = from_z.shape[0] // 7
    block = 8 * q

    def rows(start, count):
        return pl.ds(pl.multiple_of(start, 8), count)

    def add(start, ref, count, pieces):
        where = rows(start, count)
        total = part[where, :]
        for p in range(pieces):
            total = total + ref[p * count : (p + 1) * count, :]
        return where, total

    half, plane = 16 * block, 4 * block
    copy = mail.send(part.at[rows((1 - here.k) * half, half)], from_k, here.at(dk=1))
    yield
    copy.wait_recv()
    base = here.k * half

    @pl.loop(0, 4)
    def _(i):
        where = rows(base + i * plane, plane)
        part[where, :] = part[where, :] + from_k[rows(i * plane, plane), :]

    copies = [
        mail.send(
            part.at[rows(base + (here.x + d) % 4 * plane, plane)],
            from_x.at[pl.ds((d - 1) * plane, plane)],
            here.at(dx=d),
        )
        for d in (1, 2, 3)
    ]
    yield
    for copy in copies:
        copy.wait_recv()
    base = base + here.x * plane
    where, total = add(base, from_x, plane, 3)
    part[where, :] = total
    copies = [
        mail.send(
            part.at[rows(base + (here.y + d) % 4 * block, block)],
            from_y.at[pl.ds((d - 1) * block, block)],
            here.at(dy=d),
        )
        for d in (1, 2, 3)
    ]
    yield
    for copy in copies:
        copy.wait_recv()
    base = base + here.y * block
    where, total = add(base, from_y, block, 3)
    part[where, :] = total
    copies = [
        mail.send(
            part.at[rows(base + (here.z + d) % 8 * q, q)], from_z.at[pl.ds((d - 1) * q, q)], here.at(dz=d)
        )
        for d in range(1, 8)
    ]
    yield
    for copy in copies:
        copy.wait_recv()
    _, total = add(base + here.z * q, from_z, q, 7)
    base = ((here.k * 4 + here.y) * 4 + here.x) * block
    mine = rows(base + here.z * q, q)
    out[mine, :] = total
    copies = [mail.send(out.at[mine], out.at[mine], here.at(dz=d)) for d in range(1, 8)]
    yield
    for copy in copies:
        copy.wait_recv()
    mine = out.at[rows(base, block)]
    copies = [mail.send(mine, mine, here.at(dx=d)) for d in (1, 2, 3)]
    yield
    for copy in copies:
        copy.wait_recv()
    mine = out.at[rows((here.k * 4 + here.y) * plane, plane)]
    copies = [mail.send(mine, mine, here.at(dy=d)) for d in (1, 2, 3)]
    yield
    for copy in copies:
        copy.wait_recv()
    mine = out.at[rows(here.k * half, half)]
    copy = mail.send(mine, mine, here.at(dk=1))
    yield
    copy.wait_recv()
    yield


def square(ref, block, which):
    parts = []
    for j in range(4):
        start, stop = (which * 4 + j) * B, (which * 4 + j + 1) * B
        pieces = []
        while start < stop:
            index = start // block
            end = min(stop, (index + 1) * block)
            k, x, y = index // 16, index // 4 % 4, index % 4
            at = (k * 16 + y * 4 + x) * block + start - index * block
            pieces.append(ref[at : at + end - start, :])
            start = end
        parts.append(jnp.concatenate(pieces, axis=0))
    return jnp.concatenate(parts, axis=1)


def mirror_kernel(
    h, u, t,
    s_out, sh_out, uch_out, urh_out, tch_out, trt_out, bch_out, brh_out, eh_out,
    lt, bz, bx, bs, m, uc, ur, th, eh,
    sh, uch, urh, tch, trt, bch, brh,
    e_part, e_out, e_k, e_x, e_y, e_z,
    send_sems, recv_sems, local_sems,
):
    here = Place()
    greet(
        [here.at(dx=d) for d in (1, 2, 3)]
        + [here.at(dz=d) for d in range(1, 8)]
        + [here.at(dy=d, dk=e) for d in range(4) for e in range(2) if d or e]
    )
    mail = Mail(send_sems, recv_sems)
    uc[rows48(here.f), :] = u[...]
    ur[rows48(here.slot), :] = u[...]
    row_steps, col_steps = gather_row(mail, here, uc), gather_col(mail, here, ur)
    next(row_steps)
    next(col_steps)

    for zl in range(2):
        for j in range(6):
            lt[zl, 128 * j : 128 * j + 128, :] = h[pl.ds(zl * 384 * 6 + j, 384, stride=6), :].T
    z_copies = []
    for d in range(1, 8):
        z = (here.z + d) % 8
        block = lt.at[z % 2, pl.ds(pl.multiple_of(z // 2 * 192, 8), 192)]
        z_copies.append(mail.send(block, bz.at[here.z], here.at(dz=d)))
    bz[here.z] = lt[here.zl, pl.ds(pl.multiple_of(here.zh * 192, 8), 192), :]

    for p in range(2):
        high, low = split(t[p])
        th[0, p], th[1, p] = high, low
    own_second = split(mm(split(u[:, B:]), (th[0, 1], th[1, 1])))
    part = mm(split(u[:, :B].T), own_second)
    for j in range(4):
        e_part[j * B : (j + 1) * B, :] = part[:, 128 * j : 128 * j + 128]
    e_steps = all_reduce(mail, here, e_part, e_out, e_k, e_x, e_y, e_z)
    next(e_steps)

    x_copies = {}

    def along_x(d):
        z = (here.z + 8 - d) % 8
        x_copies[d] = []
        for e in (1, 2, 3):
            x_copies[d].append(
                mail.send(bz.at[z, rows48((here.x + e) % 4)], bx.at[here.x, z], here.at(dx=e))
            )
        bx[here.x, z] = bz[z, rows48(here.x), :]

    def shuffle(zl):
        for i in range(8):
            pieces = [
                bx[x, zh * 2 + zl, :, i * W : (i + 1) * W] for zh in range(4) for x in range(4)
            ]
            bs[i % 2 * 4 + i // 2, zl] = jnp.concatenate(pieces, axis=1)
        copies = []
        for dk in range(2):
            for dy in range(4):
                source = bs.at[(here.k + dk) % 2 * 4 + (here.y + dy) % 4, zl]
                where = rows48(here.slot_of(here.k, zl, here.y))
                if dk or dy:
                    copies.append(mail.send(source, m.at[where], here.at(dy=dy, dk=dk)))
                else:
                    m[where, :] = source[...]
        return copies

    along_x(0)
    next(e_steps)
    next(row_steps)
    next(col_steps)
    next(e_steps)
    next(row_steps)
    next(e_steps)
    next(row_steps)
    next(e_steps)
    for d in (2, 6, 4):
        z_copies[d - 1].wait_recv()
        along_x(d)
    for _ in range(2):
        next(e_steps)
        next(col_steps)
    for d in (0, 2, 6, 4):
        for copy in x_copies[d]:
            copy.wait_recv()
    m_copies = shuffle(here.zl)
    next(e_steps)
    for d in (1, 7):
        z_copies[d - 1].wait_recv()
        along_x(d)
    next(e_steps)
    for d in (3, 5):
        z_copies[d - 1].wait_recv()
        along_x(d)
    for d in (1, 7, 3, 5):
        for copy in x_copies[d]:
            copy.wait_recv()
    m_copies += shuffle(1 - here.zl)
    next(row_steps)
    next(col_steps)

    e = square(e_out, 64, 0)
    put(eh, (0,), e)
    put(eh, (1,), e.T)

    def bases(src, uh, bh, turned):
        @pl.loop(0, 3)
        def _(i):
            rows = pl.ds(pl.multiple_of(i * 256, 256), 256)
            value = src[rows, :]
            first, second = split(value[:, :B]), split(value[:, B:])
            for p in range(2):
                uh[p, rows, :B] = first[p]
                uh[p, rows, B:] = second[p]
            put(bh, (rows, slice(None)), value[:, :B] - mm(second, (eh[0, 0], eh[1, 0]), NT))
            for p, half in ((0, first), (1, second)):
                turned(rows, p, mm(half, (th[0, p], th[1, p])))

    def as_is(rows, p, value):
        put(tch, (rows, slice(p * B, p * B + B)), value)

    def transposed(rows, p, value):
        put(trt, (slice(p * B, p * B + B), rows), value.T)

    bases(uc, uch, bch, as_is)
    bases(ur, urh, brh, transposed)
    leaving = []

    def leave(src, dst):
        copy = pltpu.make_async_copy(src, dst, local_sems.at[len(leaving)])
        copy.start()
        leaving.append(copy)

    for src, dst in (
        (uch, uch_out), (urh, urh_out), (tch, tch_out), (trt, trt_out),
        (bch, bch_out), (brh, brh_out), (eh, eh_out),
    ):
        leave(src, dst)
    for copy in m_copies:
        copy.wait_recv()

    @pl.loop(0, 16)
    def _(slot):
        tile_row = slot // 4 % 2 * 8 + slot % 4 * 2 + slot // 8
        rows = rows48(slot)
        for j in range(6):
            cols = slice(128 * j, 128 * j + 128)
            value = 0.5 * (h[pl.ds(tile_row * (6 * W) + j, W, stride=6), :] + m[rows, cols])
            m[rows, cols] = value
            put(sh, (rows, cols), value)

    leave(sh, sh_out)
    leave(m, s_out)
    for copy in leaving:
        copy.wait()
    mail.close()


def panels_kernel(
    s_in, sh_in, uch_in, urh_in, tch_in, trt_in, bch_in, brh_in, eh_in,
    out,
    s, sh, uch, urh, tch, trt, bch, brh, eh,
    xf, xh, r1, r2, r3, xc, xr, udh, dh,
    k_part, k_out, k_k, k_x, k_y, k_z,
    send_sems, recv_sems, local_sems,
):
    here = Place()
    coming = {}
    for name, src, dst in (
        ("sh", sh_in, sh), ("tch", tch_in, tch), ("trt", trt_in, trt), ("eh", eh_in, eh),
        ("urh", urh_in, urh), ("uch", uch_in, uch), ("s", s_in, s), ("bch", bch_in, bch), ("brh", brh_in, brh),
    ):
        coming[name] = pltpu.make_async_copy(src, dst, local_sems.at[len(coming)])
        coming[name].start()
    greet(
        [here.at(dx=d) for d in (1, 2, 3)]
        + [here.at(dy=d) for d in (1, 2, 3)]
        + [here.at(dz=d) for d in range(1, 8)]
        + [here.at(dk=1)]
    )
    mail = Mail(send_sems, recv_sems)
    coming["sh"].wait()
    coming["tch"].wait()

    def image(k):
        rows = pl.ds(pl.multiple_of(k * 384, 128), 384)

        @pl.loop(0, 4)
        def _(j):
            cols = pl.ds(pl.multiple_of(j * 256, 256), 256)
            value = mm(hl(sh, rows, slice(None)), hl(tch, slice(None), cols))
            xf[rows, cols] = value
            put(xh, (rows, cols), value)

        return xf.at[rows]

    x_core = mail.send(image(1 - here.k), r1, here.at(dk=1))
    image(here.k)
    x_core.wait_recv()

    @pl.loop(0, 8)
    def _(i):
        r1[rows48(i), :] = r1[rows48(i), :] + xf[rows48(here.k * 8 + i), :]

    x_y = []
    for d in (1, 2, 3):
        for zl in range(2):
            x_y.append(
                mail.send(r1.at[rows48(zl * 4 + (here.y + d) % 4)], r2.at[d - 1, zl], here.at(dy=d))
            )

    coming["trt"].wait()

    @pl.loop(0, 6)
    def _(i):
        which = i // 2
        left = pl.ds(pl.multiple_of(which // 2 * B, B), B)
        cols = pl.ds(pl.multiple_of((which + 1) // 2 * B + i % 2 * 256, 256), 256)
        value = mm(hl(trt, left, slice(None)), hl(xh, slice(None), cols))
        for j in range(2):
            k_part[pl.ds(pl.multiple_of((i * 2 + j) * B, B), B), :] = value[:, 128 * j : 128 * j + 128]

    k_steps = all_reduce(mail, here, k_part, k_out, k_k, k_x, k_y, k_z)
    next(k_steps)
    next(k_steps)
    for copy in x_y:
        copy.wait_recv()
    for zl in range(2):
        where = rows48(zl * 4 + here.y)
        r1[where, :] = r1[where, :] + (r2[0, zl] + r2[1, zl] + r2[2, zl])
    x_z = mail.send(r1.at[rows48((1 - here.zl) * 4 + here.y)], r3, here.zl_peer())
    next(k_steps)
    x_z.wait_recv()
    piece = r1[rows48(here.zl * 4 + here.y), :] + r3[...]
    xc[rows48(here.f), :] = piece
    xr[rows48(here.slot), :] = piece
    row_steps, col_steps = gather_row(mail, here, xc), gather_col(mail, here, xr)
    next(row_steps)
    next(col_steps)
    next(k_steps)
    next(k_steps)
    next(col_steps)
    next(k_steps)
    next(row_steps)
    next(k_steps)
    next(row_steps)
    next(row_steps)
    next(col_steps)
    next(col_steps)
    next(k_steps)
    next(k_steps)

    for name in ("eh", "urh", "uch", "s"):
        coming[name].wait()
    z1 = square(k_out, 192, 0)
    k12 = square(k_out, 192, 1)
    z1e = mm(split(z1), (eh[0, 0], eh[1, 0]))
    turned = mm((eh[0, 1], eh[1, 1]), split(k12 - 0.5 * z1e))
    z2 = square(k_out, 192, 2) - (turned + turned.T)
    corner = z1e - k12
    put(dh, (slice(0, B), slice(0, B)), -z1)
    put(dh, (slice(0, B), slice(B, U)), corner)
    put(dh, (slice(B, U), slice(0, B)), corner.T)
    put(dh, (slice(B, U), slice(B, U)), -z2)

    @pl.loop(0, 4)
    def _(j):
        cols = pl.ds(pl.multiple_of(j * 256, 256), 256)
        put(udh, (slice(None), cols), mm(hl(urh, slice(None), slice(None)), hl(dh, slice(None), cols)))

    @pl.loop(0, 3)
    def _(j):
        cols = pl.ds(pl.multiple_of(j * 256, 256), 256)
        s[:, cols] = s[:, cols] - mm(hl(udh, slice(None), slice(None)), hl(uch, cols, slice(None)), NT)

    coming["bch"].wait()
    coming["brh"].wait()
    next(col_steps)
    next(row_steps)

    @pl.loop(0, 3)
    def _(i):
        rows = pl.ds(pl.multiple_of(i * 256, 256), 256)
        put(xh, (rows, slice(None)), xr[rows, :])
        put(tch, (rows, slice(None)), xc[rows, :])

    one, two, every = slice(0, B), slice(B, U), slice(None)

    @pl.loop(0, 3)
    def _(j):
        cols = pl.ds(pl.multiple_of(j * 256, 256), 256)
        value = s[:, cols] - mm(hl(xh, every, one), hl(bch, cols, every), NT)
        value = value - mm(hl(xh, every, two), hl(uch, cols, two), NT)
        value = value - mm(hl(brh, every, every), hl(tch, cols, one), NT)
        value = value - mm(hl(urh, every, two), hl(tch, cols, two), NT)
        for slot in range(16):
            tile_row = slot // 4 % 2 * 8 + slot % 4 * 2 + slot // 8
            for e in range(2):
                where = pl.ds(tile_row * (6 * W) + j * 2 + e, W, stride=6)
                out[where, :] = value[slot * W : (slot + 1) * W, 128 * e : 128 * e + 128]

    mail.close()


def vmem(*shape, dtype=F32):
    return pltpu.VMEM(shape, dtype)


def on_device(hessian, panels, factors):
    tile = hessian.reshape(M * 6, 128)
    piece = panels.reshape(W, U)
    in_vmem, anywhere = pl.BlockSpec(memory_space=pltpu.VMEM), pl.BlockSpec(memory_space=pl.ANY)
    shapes = [
        ((M, M), F32), ((2, M, M), BF16), ((2, M, U), BF16), ((2, M, U), BF16), ((2, M, U), BF16),
        ((2, U, M), BF16), ((2, M, B), BF16), ((2, M, B), BF16), ((2, 2, B, B), BF16),
    ]
    sums = lambda q: [vmem(256 * q, 128), vmem(128 * q, 128), vmem(96 * q, 128), vmem(24 * q, 128), vmem(7 * q, 128)]
    sems = pltpu.SemaphoreType.DMA
    middle = pl.pallas_call(
        mirror_kernel,
        name="mirror",
        out_shape=[jax.ShapeDtypeStruct(*shape) for shape in shapes],
        in_specs=[in_vmem] * 3,
        out_specs=[anywhere] * 9,
        scratch_shapes=[
            vmem(2, M, 384), vmem(8, 192, 384), vmem(4, 8, W, 384), vmem(8, 2, W, M), vmem(M, M),
            vmem(M, U), vmem(M, U), vmem(2, 2, B, B, dtype=BF16), vmem(2, 2, B, B, dtype=BF16),
            *[vmem(*shape, dtype=dtype) for shape, dtype in shapes[1:8]],
            vmem(2048, 128), *sums(8),
            sems((104,)), sems((104,)), sems((9,)),
        ],
        compiler_params=pltpu.CompilerParams(
            collective_id=0, has_side_effects=True, vmem_limit_bytes=60 << 20
        ),
    )(tile, piece, factors)
    updated = pl.pallas_call(
        panels_kernel,
        name="panels",
        out_shape=jax.ShapeDtypeStruct((M * 6, 128), F32),
        in_specs=[anywhere] * 9,
        out_specs=in_vmem,
        scratch_shapes=[
            *[vmem(*shape, dtype=dtype) for shape, dtype in shapes],
            vmem(M, U), vmem(2, M, U, dtype=BF16), vmem(M // 2, U), vmem(3, 2, W, U), vmem(W, U),
            vmem(M, U), vmem(M, U), vmem(2, M, U, dtype=BF16), vmem(2, U, U, dtype=BF16),
            vmem(6144, 128), *sums(24),
            sems((72,)), sems((72,)), sems((9,)),
        ],
        compiler_params=pltpu.CompilerParams(
            collective_id=1, has_side_effects=True, vmem_limit_bytes=62 << 20
        ),
    )(*middle)
    return updated.reshape(1, M, 1, M)


def solution(mesh):
    return jax.shard_map(
        on_device,
        mesh=mesh,
        in_specs=(P("row", None, "col", None), P("row", "col", None, None), P()),
        out_specs=P("row", None, "col", None),
        check_vma=False,
    )
```

```python
import jax
import jax.numpy as jnp
from jax import lax
from jax.experimental import pallas as pl
from jax.experimental.pallas import tpu as pltpu
from jax.sharding import PartitionSpec as P

MESH = pl.DeviceIdType.MESH
F32, BF16 = jnp.float32, jnp.bfloat16
NX, NY, NZ = 4, 4, 8
W = 48
M = 768
B = 512
U = 2 * B


def split(value):
    high = value.astype(BF16)
    return high, (value - high.astype(F32)).astype(BF16)


def put(ref, where, value):
    high, low = split(value)
    ref[(0,) + where] = high
    ref[(1,) + where] = low


def mm(left, right, dims=((1,), (0,))):
    def one(a, b):
        return lax.dot_general(a, b, (dims, ((), ())), preferred_element_type=F32)

    return one(left[0], right[0]) + (one(left[0], right[1]) + one(left[1], right[0]))


NT = ((1,), (1,))


def hl(ref, *where):
    return ref[(0,) + where], ref[(1,) + where]


class Place:
    def __init__(self):
        row, col = lax.axis_index("row"), lax.axis_index("col")
        self.zh, self.x = row // NX, row % NX
        self.zl, self.y, self.k = col // (2 * NY), (col // 2) % NY, col % 2
        self.z = self.zh * 2 + self.zl
        self.f = row
        self.slot = self.slot_of(self.k, self.zl, self.y)

    def slot_of(self, k, zl, y):
        return k * 8 + zl * 4 + y

    def at(self, dx=0, dy=0, dz=0, dk=0):
        x, y, z = (self.x + dx) % NX, (self.y + dy) % NY, (self.z + dz) % NZ
        k = (self.k + dk) % 2
        return {"row": (z // 2) * NX + x, "col": (z % 2) * 2 * NY + y * 2 + k}

    def zl_peer(self):
        return {"col": (1 - self.zl) * 2 * NY + self.y * 2 + self.k, "row": self.f}


class Mail:
    def __init__(self, send_sems, recv_sems):
        self.send_sems, self.recv_sems, self.open, self.count = send_sems, recv_sems, [], 0

    def send(self, src, dst, target):
        index = self.count
        self.count += 1
        copy = pltpu.make_async_remote_copy(
            src, dst, self.send_sems.at[index], self.recv_sems.at[index], device_id=target, device_id_type=MESH
        )
        copy.start()
        self.open.append(copy)
        return copy

    def settle(self, copies=None):
        leaving = list(self.open if copies is None else copies)
        for copy in leaving:
            copy.wait_send()
        self.open = [copy for copy in self.open if not any(copy is other for other in leaving)]


def greet(partners):
    barrier = pltpu.get_barrier_semaphore()
    for target in partners:
        pl.semaphore_signal(barrier, inc=1, device_id=target, device_id_type=MESH)
    pl.semaphore_wait(barrier, len(partners))


def rows48(slot):
    return pl.ds(pl.multiple_of(slot * W, 8), W)


def logged(mail, log):
    def send(*args):
        log.append(mail.send(*args))
        return log[-1]

    return send


def gather_row(mail, here, buf, log):
    send = logged(mail, log)

    def block(zh, x):
        return buf.at[rows48(zh * NX + x)]

    mine = block(here.zh, here.x)
    far = [send(mine, mine, here.at(dz=2 * d)) for d in (1, 2, 3)]
    last = [send(mine, mine, here.at(dx=d)) for d in (1, 2, 3)]
    yield
    for d in (1, 2, 3):
        far[d - 1].wait_recv()
        got = block((here.zh + 4 - d) % 4, here.x)
        last += [send(got, got, here.at(dx=e)) for e in (1, 2, 3)]
        yield
    for copy in last:
        copy.wait_recv()
    yield


def gather_col(mail, here, buf, log):
    send = logged(mail, log)

    def block(zl):
        return buf.at[rows48(here.slot_of(here.k, zl, here.y))]

    mine = block(here.zl)
    pair = send(mine, mine, here.zl_peer())
    first = [send(mine, mine, here.at(dy=d)) for d in (1, 2, 3)]
    yield
    pair.wait_recv()
    got = block(1 - here.zl)
    second = [send(got, got, here.at(dy=d)) for d in (1, 2, 3)]
    yield
    last = []
    for zl, copies in ((here.zl, first), (1 - here.zl, second)):
        for copy in copies:
            copy.wait_recv()
        part = buf.at[pl.ds(pl.multiple_of((here.k * 8 + zl * 4) * W, 8), 4 * W)]
        last.append(send(part, part, here.at(dk=1)))
        yield
    for copy in last:
        copy.wait_recv()
    yield


def all_reduce(mail, here, part, out, from_k, from_y, from_x, from_z, swap):
    half = part.shape[0] // 2
    plane, block = half // 4, half // 16

    def rows(start, count):
        return pl.ds(pl.multiple_of(start, 8), count)

    def lanes(z):
        return pl.ds(pl.multiple_of(z * 128, 128), 128)

    def add(where, ref, count):
        total = part[where, :]
        for p in range(3):
            total = total + ref[p * count : (p + 1) * count, :]
        part[where, :] = total

    copy = mail.send(part.at[rows((1 - here.k) * half, half)], from_k, here.at(dk=1))
    yield
    copy.wait_recv()
    base = here.k * half

    @pl.loop(0, 4)
    def _(i):
        where = rows(base + i * plane, plane)
        part[where, :] = part[where, :] + from_k[rows(i * plane, plane), :]

    copies = [
        mail.send(
            part.at[rows(base + (here.y + d) % 4 * plane, plane)],
            from_y.at[pl.ds((d - 1) * plane, plane)],
            here.at(dy=d),
        )
        for d in (1, 2, 3)
    ]
    yield
    for copy in copies:
        copy.wait_recv()
    base = base + here.y * plane
    add(rows(base, plane), from_y, plane)
    copies = [
        mail.send(
            part.at[rows(base + (here.x + d) % 4 * block, block)],
            from_x.at[pl.ds((d - 1) * block, block)],
            here.at(dx=d),
        )
        for d in (1, 2, 3)
    ]
    yield
    for copy in copies:
        copy.wait_recv()
    where = rows(base + here.x * block, block)
    add(where, from_x, block)
    copies = [
        mail.send(
            part.at[where, lanes((here.z + d) % 8)], from_z.at[pl.ds((d - 1) * block, block)], here.at(dz=d)
        )
        for d in range(1, 8)
    ]
    yield
    for copy in copies:
        copy.wait_recv()
    total = part[where, lanes(here.z)]
    for p in range(7):
        total = total + from_z[p * block : (p + 1) * block, :]
    outer, inner = (here.x, here.y) if swap else (here.y, here.x)
    base = (here.k * 4 + outer) * plane
    where = rows(base + inner * block, block)
    out[where, lanes(here.z)] = total
    mine = out.at[where, lanes(here.z)]
    copies = [mail.send(mine, mine, here.at(dz=d)) for d in range(1, 8)]
    yield
    for copy in copies:
        copy.wait_recv()
    mine = out.at[where]
    copies = [mail.send(mine, mine, here.at(dy=d) if swap else here.at(dx=d)) for d in (1, 2, 3)]
    yield
    for copy in copies:
        copy.wait_recv()
    mine = out.at[rows(base, plane)]
    copies = [mail.send(mine, mine, here.at(dx=d) if swap else here.at(dy=d)) for d in (1, 2, 3)]
    yield
    for copy in copies:
        copy.wait_recv()
    mine = out.at[rows(here.k * half, half)]
    copy = mail.send(mine, mine, here.at(dk=1))
    yield
    copy.wait_recv()
    yield


def columns(j):
    return pl.ds(pl.multiple_of(j * 256, 256), 256)


EVERY, ONE, TWO = slice(None), slice(0, B), slice(B, U)


def kernel(
    h, u, t, out,
    hb, lt, bz, bx, m, uc, ur, th,
    uch, urh, p0, p1, p2, bch, brh,
    e_part, e_out, e_k, e_y, e_x, e_z,
    xt, q1, q2, r1, r2, r3,
    k_part, k_out, k_k, k_y, k_x, k_z,
    send_sems, recv_sems, local_sems,
):
    here = Place()
    loads = [
        pltpu.make_async_copy(t.at[0], xt.at[pl.ds(0, B), pl.ds(0, B)], local_sems.at[0]),
        pltpu.make_async_copy(t.at[1], xt.at[pl.ds(0, B), pl.ds(B, B)], local_sems.at[1]),
        pltpu.make_async_copy(h, hb, local_sems.at[2]),
    ]
    for copy in loads:
        copy.start()
    greet(
        [here.at(dx=d) for d in (1, 2, 3)]
        + [here.at(dz=d) for d in range(1, 8)]
        + [here.at(dy=d, dk=e) for d in range(4) for e in range(2) if d or e]
    )
    mail = Mail(send_sems, recv_sems)
    uc[rows48(here.f), :] = u[...]
    ur[rows48(here.slot), :] = u[...]
    row_log, col_log = [], []
    row_steps, col_steps = gather_row(mail, here, uc, row_log), gather_col(mail, here, ur, col_log)
    next(row_steps)
    next(col_steps)

    loads[0].wait()
    loads[1].wait()
    for p in range(2):
        high, low = split(xt[:B, p * B : p * B + B])
        th[0, p], th[1, p] = high, low
    own_second = split(mm(split(u[:, B:]), (th[0, 1], th[1, 1])))
    part = mm(split(u[:, :B].T), own_second)
    e_part[:, :B] = part[:256]
    e_part[:, B:] = part[256:]
    e_steps = all_reduce(mail, here, e_part, e_out, e_k, e_y, e_x, e_z, False)
    next(e_steps)
    next(col_steps)

    loads[2].wait()
    for zl in range(2):
        for j in range(6):
            pieces = [
                hb[pl.ds((zl * 8 + y * 2 + k) * 6 * W + j, W, stride=6), :] for k in range(2) for y in range(4)
            ]
            lt[zl, 128 * j : 128 * j + 128, :] = jnp.concatenate(pieces, axis=0).T
    next(e_steps)
    next(row_steps)
    next(row_steps)
    next(row_steps)
    z_copies = []
    for d in (2, 6, 4, 1, 7, 3, 5):
        z = (here.z + d) % 8
        block = lt.at[z % 2, pl.ds(pl.multiple_of(z // 2 * 192, 8), 192)]
        z_copies.append((d, mail.send(block, bz.at[here.z], here.at(dz=d))))
    z_copies = dict(z_copies)
    bz[here.z] = lt[here.zl, pl.ds(pl.multiple_of(here.zh * 192, 8), 192), :]
    next(e_steps)
    next(col_steps)
    next(e_steps)
    next(col_steps)
    next(e_steps)
    next(col_steps)

    def bases(src, uh, turned):
        @pl.loop(0, 3)
        def _(i):
            rows = columns(i)
            for p in range(2):
                half = split(src[rows, p * B : p * B + B])
                uh[0, rows, p * B : p * B + B] = half[0]
                uh[1, rows, p * B : p * B + B] = half[1]
                turned(rows, p, mm(half, (th[0, p], th[1, p])))

    def row_side(rows, p, value):
        put(p0, (rows, slice(p * B, p * B + B)), value)
        put(p2, (slice(p * B, p * B + B), rows), value.T)

    def col_side(rows, p, value):
        put(p1, (rows, slice(p * B, p * B + B)), value)

    bases(ur, urh, row_side)

    @pl.loop(0, 2)
    def _(i):
        rows = pl.ds(pl.multiple_of(i * 384, 128), 384)
        pieces = [lt[zl, rows, k * 192 : k * 192 + 192] for k in range(2) for zl in range(2)]
        put(p1, (slice(0, 384), slice(0, M)), jnp.concatenate(pieces, axis=1))

        @pl.loop(0, 4)
        def _(j):
            xt[rows, columns(j)] = mm(hl(p1, slice(0, 384), slice(0, M)), hl(p0, EVERY, columns(j)))

    mail.settle(col_log)
    t_x = []
    for e in (1, 2, 3):
        for zh in range(4):
            t_x.append(mail.send(xt.at[rows48(zh * 4 + (here.x + e) % 4)], q1.at[e - 1, zh], here.at(dx=e)))
    next(e_steps)
    next(row_steps)
    bases(uc, uch, col_side)
    mail.settle(row_log)

    def image(k):
        rows = pl.ds(pl.multiple_of(k * 384, 128), 384)
        for zl in range(2):
            for y in range(4):
                for j in range(6):
                    start = (zl * 8 + y * 2 + k) * 6 * W + j
                    at = (zl * 4 + y) * W
                    put(p0, (slice(at, at + W), slice(128 * j, 128 * j + 128)), hb[pl.ds(start, W, stride=6), :])

        @pl.loop(0, 4)
        def _(j):
            uc[rows, columns(j)] = mm(hl(p0, slice(0, 384), slice(0, M)), hl(p1, EVERY, columns(j)))

        return uc.at[rows]

    x_core = mail.send(image(1 - here.k), r1, here.at(dk=1))
    image(here.k)

    for j in range(4):
        right = split(uc[:, 256 * j : 256 * j + 256])
        c = j % 2
        where = slice(B + 256 * c, B + 256 * c + 256)
        value = mm(hl(p2, ONE, EVERY), right)
        if j < 2:
            k_part[:B, 256 * c : 256 * c + 256] = value
        else:
            k_part[:B, where] = k_part[:B, where] + 0.5 * value
        value = mm(hl(p2, TWO, EVERY), right)
        if j < 2:
            k_part[256 * c : 256 * c + 256, B:] = 0.5 * value.T
        else:
            k_part[B:, 256 * c : 256 * c + 256] = value[:256]
            k_part[B:, where] = value[256:]
    k_steps = all_reduce(mail, here, k_part, k_out, k_k, k_y, k_x, k_z, True)
    next(k_steps)
    x_core.wait_recv()
    mail.settle([x_core])

    @pl.loop(0, 8)
    def _(i):
        r1[rows48(i), :] = r1[rows48(i), :] + uc[rows48(here.k * 8 + i), :]

    x_y = []
    for d in (1, 2, 3):
        for zl in range(2):
            x_y.append(
                mail.send(r1.at[rows48(zl * 4 + (here.y + d) % 4)], r2.at[d - 1, zl], here.at(dy=d))
            )
    next(k_steps)
    next(e_steps)
    next(e_steps)
    next(e_steps)

    x_copies = {}

    def along_x(d):
        z = (here.z + 8 - d) % 8
        x_copies[d] = []
        for e in (1, 2, 3):
            x_copies[d].append(
                mail.send(bz.at[z, rows48((here.x + e) % 4)], bx.at[here.x, z], here.at(dx=e))
            )
        bx[here.x, z] = bz[z, rows48(here.x), :]

    def shuffle(zl):
        for i in range(8):
            for half in range(2):
                pieces = [
                    bx[x, (half * 2 + zh) * 2 + zl, :, i * W : (i + 1) * W] for zh in range(2) for x in range(4)
                ]
                lt[half, rows48(zl * 8 + i), :] = jnp.concatenate(pieces, axis=1)
        copies = []
        where = rows48(here.slot_of(here.k, zl, here.y))
        for dk in range(2):
            for dy in range(4):
                rows = rows48(zl * 8 + (here.k + dk) % 2 * 4 + (here.y + dy) % 4)
                if dk or dy:
                    copies.append(mail.send(lt.at[:, rows], m.at[:, where], here.at(dy=dy, dk=dk)))
                else:
                    m[:, where, :] = lt[:, rows, :]
        return copies

    e = jnp.concatenate([e_out[:, :B], e_out[:, B:]], axis=0)
    for p, value in ((0, e), (1, e.T)):
        high, low = split(value)
        th[0, p], th[1, p] = high, low

    def less(uh, bh):
        @pl.loop(0, 3)
        def _(i):
            rows = columns(i)
            first = uh[0, rows, ONE].astype(F32) + uh[1, rows, ONE].astype(F32)
            put(bh, (rows, EVERY), first - mm(hl(uh, rows, TWO), (th[0, 0], th[1, 0]), NT))

    less(uch, bch)
    less(urh, brh)

    along_x(0)
    for d in (2, 6, 4):
        z_copies[d].wait_recv()
        along_x(d)
    for copy in t_x:
        copy.wait_recv()
    for zh in range(4):
        where = rows48(zh * 4 + here.x)
        xt[where, :] = xt[where, :] + (q1[0, zh] + q1[1, zh] + q1[2, zh])
    t_z = [
        mail.send(xt.at[rows48((here.zh + d) % 4 * 4 + here.x)], q2.at[d - 1], here.at(dz=2 * d))
        for d in (1, 2, 3)
    ]
    for copy in x_y:
        copy.wait_recv()
    for zl in range(2):
        where = rows48(zl * 4 + here.y)
        r1[where, :] = r1[where, :] + (r2[0, zl] + r2[1, zl] + r2[2, zl])
    x_z = mail.send(r1.at[rows48((1 - here.zl) * 4 + here.y)], r3, here.zl_peer())
    next(k_steps)
    for d in (1, 7, 3, 5):
        z_copies[d].wait_recv()
        along_x(d)
    mail.settle(z_copies.values())
    for d in (0, 2, 6, 4):
        for copy in x_copies[d]:
            copy.wait_recv()
    m_copies = shuffle(here.zl)
    next(k_steps)
    x_z.wait_recv()
    for copy in t_z:
        copy.wait_recv()
    piece = r1[rows48(here.zl * 4 + here.y), :] + r3[...]
    piece = 0.5 * (piece + xt[rows48(here.f), :] + (q2[0] + q2[1] + q2[2]))
    xr, xc = uc, ur
    xc[rows48(here.f), :] = piece
    xr[rows48(here.slot), :] = piece
    row_steps, col_steps = gather_row(mail, here, xc, []), gather_col(mail, here, xr, [])
    next(row_steps)
    next(col_steps)
    next(k_steps)
    next(k_steps)
    next(col_steps)
    next(k_steps)
    next(row_steps)
    next(row_steps)
    next(row_steps)
    for d in (1, 7, 3, 5):
        for copy in x_copies[d]:
            copy.wait_recv()
    m_copies += shuffle(1 - here.zl)
    next(col_steps)
    next(col_steps)
    next(k_steps)
    next(k_steps)
    mail.settle()

    @pl.loop(0, 32)
    def _(i):
        k, y, x = i // 16, i // 4 % 4, i % 4
        k_part[pl.ds(pl.multiple_of(i * 24, 8), 24), :] = k_out[
            pl.ds(pl.multiple_of((k * 16 + x * 4 + y) * 24, 8), 24), :
        ]

    k_part[:B, :B] = 0.5 * (k_part[:B, :B] + k_part[:B, :B].T)

    @pl.loop(0, 2)
    def _(c):
        cols, right = columns(c), columns(c + 2)
        z1e = mm(split(k_part[:B, :B]), (th[0, 0, :, cols], th[1, 0, :, cols]))
        k12 = k_part[:B, right]
        xt[:B, right] = z1e - k12
        turned = mm((th[0, 1], th[1, 1]), split(k12 - 0.5 * z1e))
        k_part[B:, cols] = 0.5 * k_part[B:, cols] - turned[:256]
        k_part[B:, right] = 0.5 * k_part[B:, right] - turned[256:]

    xt[:B, :B] = -k_part[:B, :B]
    for c, ref, rows in ((0, xt, slice(B, M)), (1, e_part, slice(0, 256))):
        cols, right = slice(256 * c, 256 * c + 256), slice(B + 256 * c, B + 256 * c + 256)
        ref[rows, :B] = xt[:B, right].T
        turned = jnp.concatenate([k_part[B:, cols].T, k_part[B:, right].T], axis=1)
        ref[rows, B:] = -(k_part[B:, B * c : B * c + B] + turned)
    for i in range(4):
        rows = xt[256 * i : 256 * i + 256, :] if i < 3 else e_part[...]
        put(p2, (slice(256 * i, 256 * i + 256), EVERY), mm(split(rows), hl(uch, EVERY, EVERY), NT))

    def add_to_tile(j, scale, value):
        for slot in range(16):
            tile_row = slot // 4 % 2 * 8 + slot % 4 * 2 + slot // 8
            for e in range(2):
                where = pl.ds(tile_row * (6 * W) + j * 2 + e, W, stride=6)
                hb[where, :] = scale * hb[where, :] - value[slot * W : (slot + 1) * W, 128 * e : 128 * e + 128]

    @pl.loop(0, 3)
    def _(j):
        add_to_tile(j, 0.5, mm(hl(urh, EVERY, EVERY), hl(p2, EVERY, columns(j))))

    next(col_steps)
    next(row_steps)

    @pl.loop(0, 3)
    def _(i):
        put(p0, (columns(i), EVERY), xr[columns(i), :])
        put(p1, (columns(i), EVERY), xc[columns(i), :])

    @pl.loop(0, 3)
    def _(j):
        rows = columns(j)
        value = mm(hl(p0, EVERY, ONE), hl(bch, rows, EVERY), NT)
        value = value + mm(hl(p0, EVERY, TWO), hl(uch, rows, TWO), NT)
        value = value + mm(hl(brh, EVERY, EVERY), hl(p1, rows, ONE), NT)
        value = value + mm(hl(urh, EVERY, TWO), hl(p1, rows, TWO), NT)
        add_to_tile(j, 1.0, value)

    for copy in m_copies:
        copy.wait_recv()

    @pl.loop(0, 16)
    def _(slot):
        tile_row = slot // 4 % 2 * 8 + slot % 4 * 2 + slot // 8
        for j in range(6):
            where = pl.ds(tile_row * (6 * W) + j, W, stride=6)
            hb[where, :] = hb[where, :] + 0.5 * m[j // 3, rows48(slot), 128 * (j % 3) : 128 * (j % 3) + 128]

    mail.settle()
    last = pltpu.make_async_copy(hb, out, local_sems.at[3])
    last.start()
    last.wait()


def vmem(*shape, dtype=F32):
    return pltpu.VMEM(shape, dtype)


def on_device(hessian, panels, factors):
    anywhere = pl.BlockSpec(memory_space=pl.ANY)

    def sums(rows):
        return [vmem(rows, U), vmem(rows, U), vmem(rows // 2, U), vmem(rows * 3 // 8, U),
                vmem(rows * 3 // 32, U), vmem(rows * 7 // 32, 128)]

    updated = pl.pallas_call(
        kernel,
        name="panels",
        out_shape=jax.ShapeDtypeStruct((M * 6, 128), F32),
        in_specs=[anywhere, pl.BlockSpec(memory_space=pltpu.VMEM), anywhere],
        out_specs=anywhere,
        scratch_shapes=[
            vmem(M * 6, 128), vmem(2, M, 384), vmem(8, 192, 384), vmem(4, 8, W, 384), vmem(2, M, 384),
            vmem(M, U), vmem(M, U), vmem(2, 2, B, B, dtype=BF16),
            *[vmem(2, M, U, dtype=BF16)] * 4, vmem(2, U, M, dtype=BF16), *[vmem(2, M, B, dtype=BF16)] * 2,
            *sums(256),
            vmem(M, U), vmem(3, 4, W, U), vmem(3, W, U), vmem(M // 2, U), vmem(3, 2, W, U), vmem(W, U),
            *sums(M),
            pltpu.SemaphoreType.DMA((176,)), pltpu.SemaphoreType.DMA((176,)), pltpu.SemaphoreType.DMA((4,)),
        ],
        compiler_params=pltpu.CompilerParams(
            collective_id=0, has_side_effects=True, vmem_limit_bytes=63 << 20
        ),
    )(hessian.reshape(M * 6, 128), panels.reshape(W, U), factors)
    return updated.reshape(1, M, 1, M)


def solution(mesh):
    return jax.shard_map(
        on_device,
        mesh=mesh,
        in_specs=(P("row", None, "col", None), P("row", "col", None, None), P()),
        out_specs=P("row", None, "col", None),
        check_vma=False,
    )
```

```python
import jax
import jax.numpy as jnp
from jax import lax
from jax.experimental import pallas as pl
from jax.experimental.pallas import tpu as pltpu
from jax.sharding import PartitionSpec as P

MESH = pl.DeviceIdType.MESH
F32, BF16 = jnp.float32, jnp.bfloat16
NX, NY, NZ = 4, 4, 8
W = 48
M = 768
B = 512
U = 2 * B


def split(value):
    high = value.astype(BF16)
    return high, (value - high.astype(F32)).astype(BF16)


def put(ref, where, value):
    high, low = split(value)
    ref[(0,) + where] = high
    ref[(1,) + where] = low


def mm(left, right, dims=((1,), (0,))):
    def one(a, b):
        return lax.dot_general(a, b, (dims, ((), ())), preferred_element_type=F32)

    return one(left[0], right[0]) + (one(left[0], right[1]) + one(left[1], right[0]))


NT = ((1,), (1,))


def hl(ref, *where):
    return ref[(0,) + where], ref[(1,) + where]


class Place:
    def __init__(self):
        row, col = lax.axis_index("row"), lax.axis_index("col")
        self.zh, self.x = row // NX, row % NX
        self.zl, self.y, self.k = col // (2 * NY), (col // 2) % NY, col % 2
        self.z = self.zh * 2 + self.zl
        self.f = row
        self.slot = self.slot_of(self.k, self.zl, self.y)

    def slot_of(self, k, zl, y):
        return k * 8 + zl * 4 + y

    def at(self, dx=0, dy=0, dz=0, dk=0):
        x, y, z = (self.x + dx) % NX, (self.y + dy) % NY, (self.z + dz) % NZ
        k = (self.k + dk) % 2
        return {"row": (z // 2) * NX + x, "col": (z % 2) * 2 * NY + y * 2 + k}

    def zl_peer(self):
        return {"col": (1 - self.zl) * 2 * NY + self.y * 2 + self.k, "row": self.f}


class Mail:
    def __init__(self, send_sems, recv_sems):
        self.send_sems, self.recv_sems, self.open, self.count = send_sems, recv_sems, [], 0

    def send(self, src, dst, target):
        index = self.count
        self.count += 1
        copy = pltpu.make_async_remote_copy(
            src, dst, self.send_sems.at[index], self.recv_sems.at[index], device_id=target, device_id_type=MESH
        )
        copy.start()
        self.open.append(copy)
        return copy

    def settle(self, copies=None):
        leaving = list(self.open if copies is None else copies)
        for copy in leaving:
            copy.wait_send()
        self.open = [copy for copy in self.open if not any(copy is other for other in leaving)]


def greet(partners):
    barrier = pltpu.get_barrier_semaphore()
    for target in partners:
        pl.semaphore_signal(barrier, inc=1, device_id=target, device_id_type=MESH)
    pl.semaphore_wait(barrier, len(partners))


def rows48(slot):
    return pl.ds(pl.multiple_of(slot * W, 8), W)


def logged(mail, log):
    def send(*args):
        log.append(mail.send(*args))
        return log[-1]

    return send


def gather_row(mail, here, buf, log):
    send = logged(mail, log)
    halves = []

    def block(zh, x):
        return buf.at[rows48(zh % 4 * NX + x % NX)]

    def half(zh, x, which):
        return buf.at[rows48(zh % 4 * NX + x % NX), pl.ds(which * B, B)]

    def both(zh):
        mine = block(zh, here.x)
        return zh, send(mine, mine, here.at(dx=1)), send(mine, mine, here.at(dx=3))

    def pass_on(zh, from_left, from_right):
        from_left.wait_recv()
        part = half(zh, here.x + 3, 0)
        halves.append(send(part, part, here.at(dx=1)))
        from_right.wait_recv()
        part = half(zh, here.x + 1, 1)
        halves.append(send(part, part, here.at(dx=3)))

    mine = block(here.zh, here.x)
    far = {d: send(mine, mine, here.at(dz=2 * d)) for d in (1, 3)}
    group = both(here.zh)
    yield
    for d in (1, 3, 2):
        far[d].wait_recv()
        if d == 1:
            far[2] = send(mine, mine, here.at(dz=4))
        later = both(here.zh + 4 - d)
        pass_on(*group)
        group = later
        yield
    pass_on(*group)
    yield
    for copy in halves:
        copy.wait_recv()
    yield


def gather_col(mail, here, buf, log):
    send = logged(mail, log)

    def block(zl):
        return buf.at[rows48(here.slot_of(here.k, zl, here.y))]

    mine = block(here.zl)
    pair = send(mine, mine, here.zl_peer())
    first = [send(mine, mine, here.at(dy=d)) for d in (1, 2, 3)]
    yield
    pair.wait_recv()
    got = block(1 - here.zl)
    second = [send(got, got, here.at(dy=d)) for d in (1, 2, 3)]
    yield
    last = []
    for zl, copies in ((here.zl, first), (1 - here.zl, second)):
        for copy in copies:
            copy.wait_recv()
        part = buf.at[pl.ds(pl.multiple_of((here.k * 8 + zl * 4) * W, 8), 4 * W)]
        last.append(send(part, part, here.at(dk=1)))
        yield
    for copy in last:
        copy.wait_recv()
    yield


def all_reduce(mail, here, part, out, from_k, from_y, from_x, from_z, swap):
    half = part.shape[0] // 2
    plane, block = half // 4, half // 16

    def rows(start, count):
        return pl.ds(pl.multiple_of(start, 8), count)

    def lanes(z):
        return pl.ds(pl.multiple_of(z * 128, 128), 128)

    def add(where, ref, count):
        total = part[where, :]
        for p in range(3):
            total = total + ref[p * count : (p + 1) * count, :]
        part[where, :] = total

    copy = mail.send(part.at[rows((1 - here.k) * half, half)], from_k, here.at(dk=1))
    yield
    copy.wait_recv()
    base = here.k * half

    @pl.loop(0, 4)
    def _(i):
        where = rows(base + i * plane, plane)
        part[where, :] = part[where, :] + from_k[rows(i * plane, plane), :]

    copies = [
        mail.send(
            part.at[rows(base + (here.y + d) % 4 * plane, plane)],
            from_y.at[pl.ds((d - 1) * plane, plane)],
            here.at(dy=d),
        )
        for d in (1, 2, 3)
    ]
    yield
    for copy in copies:
        copy.wait_recv()
    base = base + here.y * plane
    add(rows(base, plane), from_y, plane)
    copies = [
        mail.send(
            part.at[rows(base + (here.x + d) % 4 * block, block)],
            from_x.at[pl.ds((d - 1) * block, block)],
            here.at(dx=d),
        )
        for d in (1, 2, 3)
    ]
    yield
    for copy in copies:
        copy.wait_recv()
    where = rows(base + here.x * block, block)
    add(where, from_x, block)
    copies = [
        mail.send(
            part.at[where, lanes((here.z + d) % 8)], from_z.at[pl.ds((d - 1) * block, block)], here.at(dz=d)
        )
        for d in range(1, 8)
    ]
    yield
    for copy in copies:
        copy.wait_recv()
    total = part[where, lanes(here.z)]
    for p in range(7):
        total = total + from_z[p * block : (p + 1) * block, :]
    outer, inner = (here.x, here.y) if swap else (here.y, here.x)
    base = (here.k * 4 + outer) * plane
    where = rows(base + inner * block, block)
    out[where, lanes(here.z)] = total
    mine = out.at[where, lanes(here.z)]
    copies = [mail.send(mine, mine, here.at(dz=d)) for d in range(1, 8)]
    yield
    for copy in copies:
        copy.wait_recv()
    mine = out.at[where]
    copies = [mail.send(mine, mine, here.at(dy=d) if swap else here.at(dx=d)) for d in (1, 2, 3)]
    yield
    for copy in copies:
        copy.wait_recv()
    mine = out.at[rows(base, plane)]
    copies = [mail.send(mine, mine, here.at(dx=d) if swap else here.at(dy=d)) for d in (1, 2, 3)]
    yield
    for copy in copies:
        copy.wait_recv()
    mine = out.at[rows(here.k * half, half)]
    copy = mail.send(mine, mine, here.at(dk=1))
    yield
    copy.wait_recv()
    yield


def columns(j):
    return pl.ds(pl.multiple_of(j * 256, 256), 256)


EVERY, ONE, TWO = slice(None), slice(0, B), slice(B, U)


def kernel(
    h, u, t, out,
    hb, lt, bz, bx, m, uc, ur, th,
    uch, urh, p0, p1, p2, bch, brh,
    e_part, e_out, e_k, e_y, e_x, e_z,
    xt, q0, q1, q2, r1, r2, r3,
    k_part, k_out, k_k, k_y, k_x, k_z,
    send_sems, recv_sems, local_sems,
):
    here = Place()
    loads = [
        pltpu.make_async_copy(t.at[0], xt.at[pl.ds(0, B), pl.ds(0, B)], local_sems.at[0]),
        pltpu.make_async_copy(t.at[1], xt.at[pl.ds(0, B), pl.ds(B, B)], local_sems.at[1]),
        pltpu.make_async_copy(h, hb, local_sems.at[2]),
    ]
    for copy in loads:
        copy.start()
    greet(
        [here.at(dx=d) for d in (1, 2, 3)]
        + [here.at(dz=d) for d in range(1, 8)]
        + [here.at(dy=d, dk=e) for d in range(4) for e in range(2) if d or e]
    )
    mail = Mail(send_sems, recv_sems)
    uc[rows48(here.f), :] = u[...]
    ur[rows48(here.slot), :] = u[...]
    row_log, col_log = [], []
    row_steps, col_steps = gather_row(mail, here, uc, row_log), gather_col(mail, here, ur, col_log)
    next(row_steps)
    next(col_steps)

    loads[0].wait()
    loads[1].wait()
    for p in range(2):
        high, low = split(xt[:B, p * B : p * B + B])
        th[0, p], th[1, p] = high, low
    own_second = split(mm(split(u[:, B:]), (th[0, 1], th[1, 1])))
    part = mm(split(u[:, :B].T), own_second)
    e_part[:, :B] = part[:256]
    e_part[:, B:] = part[256:]
    e_steps = all_reduce(mail, here, e_part, e_out, e_k, e_y, e_x, e_z, False)
    next(e_steps)
    next(col_steps)

    loads[2].wait()
    for zl in range(2):
        for j in range(6):
            pieces = [
                hb[pl.ds((zl * 8 + y * 2 + k) * 6 * W + j, W, stride=6), :] for k in range(2) for y in range(4)
            ]
            lt[zl, 128 * j : 128 * j + 128, :] = jnp.concatenate(pieces, axis=0).T
    next(row_steps)
    next(row_steps)
    next(row_steps)
    z_copies = {}
    for d in (2, 6, 4, 1, 7, 3, 5):
        z = (here.z + d) % 8
        block = lt.at[z % 2, pl.ds(pl.multiple_of(z // 2 * 192, 8), 192)]
        z_copies[d] = mail.send(block, bz.at[here.z], here.at(dz=d))
    bz[here.z] = lt[here.zl, pl.ds(pl.multiple_of(here.zh * 192, 8), 192), :]
    next(col_steps)
    next(row_steps)
    next(col_steps)
    next(e_steps)
    next(col_steps)

    def bases(src, uh, turned):
        @pl.loop(0, 3)
        def _(i):
            rows = columns(i)
            for p in range(2):
                half = split(src[rows, p * B : p * B + B])
                uh[0, rows, p * B : p * B + B] = half[0]
                uh[1, rows, p * B : p * B + B] = half[1]
                turned(rows, p, mm(half, (th[0, p], th[1, p])))

    def row_side(rows, p, value):
        put(p0, (rows, slice(p * B, p * B + B)), value)
        put(p2, (slice(p * B, p * B + B), rows), value.T)

    def col_side(rows, p, value):
        put(p1, (rows, slice(p * B, p * B + B)), value)

    bases(ur, urh, row_side)

    @pl.loop(0, 2)
    def _(i):
        rows = pl.ds(pl.multiple_of(i * 384, 128), 384)
        pieces = [lt[zl, rows, k * 192 : k * 192 + 192] for k in range(2) for zl in range(2)]
        put(p1, (slice(0, 384), slice(0, M)), jnp.concatenate(pieces, axis=1))

        @pl.loop(0, 4)
        def _(j):
            xt[rows, columns(j)] = mm(hl(p1, slice(0, 384), slice(0, M)), hl(p0, EVERY, columns(j)))

    mail.settle(col_log)

    def target(zh, dx):
        return rows48(zh * 4 + (here.x + dx) % 4)

    t_half = []
    for zh in range(4):
        t_half.append(mail.send(xt.at[target(zh, 2), pl.ds(0, B)], q0.at[0, zh], here.at(dx=1)))
        t_half.append(mail.send(xt.at[target(zh, 2), pl.ds(B, B)], q0.at[1, zh], here.at(dx=3)))
    next(row_steps)
    bases(uc, uch, col_side)
    mail.settle(row_log)
    for copy in t_half:
        copy.wait_recv()
    t_x = []
    for zh in range(4):
        xt[target(zh, 1), ONE] = xt[target(zh, 1), ONE] + q0[0, zh]
        xt[target(zh, 3), TWO] = xt[target(zh, 3), TWO] + q0[1, zh]
        t_x.append(mail.send(xt.at[target(zh, 1)], q1.at[0, zh], here.at(dx=1)))
        t_x.append(mail.send(xt.at[target(zh, 3)], q1.at[1, zh], here.at(dx=3)))

    def image(k):
        rows = pl.ds(pl.multiple_of(k * 384, 128), 384)
        for zl in range(2):
            for y in range(4):
                for j in range(6):
                    start = (zl * 8 + y * 2 + k) * 6 * W + j
                    at = (zl * 4 + y) * W
                    put(p0, (slice(at, at + W), slice(128 * j, 128 * j + 128)), hb[pl.ds(start, W, stride=6), :])

        @pl.loop(0, 4)
        def _(j):
            uc[rows, columns(j)] = mm(hl(p0, slice(0, 384), slice(0, M)), hl(p1, EVERY, columns(j)))

        return uc.at[rows]

    x_core = mail.send(image(1 - here.k), r1, here.at(dk=1))
    image(here.k)

    for j in range(4):
        right = split(uc[:, 256 * j : 256 * j + 256])
        c = j % 2
        where = slice(B + 256 * c, B + 256 * c + 256)
        value = mm(hl(p2, ONE, EVERY), right)
        if j < 2:
            k_part[:B, 256 * c : 256 * c + 256] = value
        else:
            k_part[:B, where] = k_part[:B, where] + 0.5 * value
        value = mm(hl(p2, TWO, EVERY), right)
        if j < 2:
            k_part[256 * c : 256 * c + 256, B:] = 0.5 * value.T
        else:
            k_part[B:, 256 * c : 256 * c + 256] = value[:256]
            k_part[B:, where] = value[256:]
    mail.settle([x_core])
    k_steps = all_reduce(mail, here, k_part, k_out, k_k, k_y, k_x, k_z, True)
    next(k_steps)
    x_core.wait_recv()

    @pl.loop(0, 8)
    def _(i):
        r1[rows48(i), :] = r1[rows48(i), :] + uc[rows48(here.k * 8 + i), :]

    x_y = []
    for d in (1, 2, 3):
        for zl in range(2):
            x_y.append(
                mail.send(r1.at[rows48(zl * 4 + (here.y + d) % 4)], r2.at[d - 1, zl], here.at(dy=d))
            )
    next(k_steps)
    next(e_steps)

    x_copies = {}

    def along_x(d):
        z = (here.z + 8 - d) % 8
        x_copies[d] = []
        for e in (1, 2, 3):
            x_copies[d].append(
                mail.send(bz.at[z, rows48((here.x + e) % 4)], bx.at[here.x, z], here.at(dx=e))
            )
        bx[here.x, z] = bz[z, rows48(here.x), :]

    def shuffle(zl):
        for i in range(8):
            for half in range(2):
                pieces = [
                    bx[x, (half * 2 + zh) * 2 + zl, :, i * W : (i + 1) * W] for zh in range(2) for x in range(4)
                ]
                lt[half, rows48(zl * 8 + i), :] = jnp.concatenate(pieces, axis=1)
        copies = []
        where = rows48(here.slot_of(here.k, zl, here.y))
        for dk in range(2):
            for dy in range(4):
                rows = rows48(zl * 8 + (here.k + dk) % 2 * 4 + (here.y + dy) % 4)
                if dk or dy:
                    copies.append(mail.send(lt.at[:, rows], m.at[:, where], here.at(dy=dy, dk=dk)))
                else:
                    m[:, where, :] = lt[:, rows, :]
        return copies

    for copy in t_x:
        copy.wait_recv()
    for zh in range(4):
        where = target(zh, 0)
        xt[where, :] = xt[where, :] + (q1[0, zh] + q1[1, zh])
    t_z = [
        mail.send(xt.at[rows48((here.zh + d) % 4 * 4 + here.x)], q2.at[d - 1], here.at(dz=2 * d))
        for d in (1, 2, 3)
    ]
    for copy in x_y:
        copy.wait_recv()
    for zl in range(2):
        where = rows48(zl * 4 + here.y)
        r1[where, :] = r1[where, :] + (r2[0, zl] + r2[1, zl] + r2[2, zl])
    x_z = mail.send(r1.at[rows48((1 - here.zl) * 4 + here.y)], r3, here.zl_peer())
    along_x(0)
    for d in (2, 6, 4, 1, 7, 3, 5):
        z_copies[d].wait_recv()
        along_x(d)
    next(e_steps)
    next(k_steps)
    mail.settle(z_copies.values())
    next(k_steps)
    next(e_steps)
    x_z.wait_recv()
    for copy in t_z:
        copy.wait_recv()
    piece = r1[rows48(here.zl * 4 + here.y), :] + r3[...]
    piece = 0.5 * (piece + xt[rows48(here.f), :] + (q2[0] + q2[1] + q2[2]))
    xr, xc = uc, ur
    xc[rows48(here.f), :] = piece
    xr[rows48(here.slot), :] = piece
    closing = list(mail.open)
    row_steps, col_steps = gather_row(mail, here, xc, []), gather_col(mail, here, xr, [])
    next(row_steps)
    next(col_steps)
    next(k_steps)
    next(e_steps)
    next(col_steps)
    next(row_steps)
    next(k_steps)
    next(e_steps)
    next(row_steps)
    next(row_steps)
    next(k_steps)
    next(e_steps)
    m_copies = []
    for zl, deltas in ((here.zl, (0, 2, 6, 4)), (1 - here.zl, (1, 7, 3, 5))):
        for d in deltas:
            for copy in x_copies[d]:
                copy.wait_recv()
        m_copies += shuffle(zl)
    next(row_steps)
    next(col_steps)
    next(col_steps)
    next(e_steps)

    e = jnp.concatenate([e_out[:, :B], e_out[:, B:]], axis=0)
    for p, value in ((0, e), (1, e.T)):
        high, low = split(value)
        th[0, p], th[1, p] = high, low

    def less(uh, bh):
        @pl.loop(0, 3)
        def _(i):
            rows = columns(i)
            first = uh[0, rows, ONE].astype(F32) + uh[1, rows, ONE].astype(F32)
            put(bh, (rows, EVERY), first - mm(hl(uh, rows, TWO), (th[0, 0], th[1, 0]), NT))

    less(uch, bch)
    less(urh, brh)

    next(k_steps)
    next(k_steps)
    mail.settle(closing)

    @pl.loop(0, 32)
    def _(i):
        k, y, x = i // 16, i // 4 % 4, i % 4
        k_part[pl.ds(pl.multiple_of(i * 24, 8), 24), :] = k_out[
            pl.ds(pl.multiple_of((k * 16 + x * 4 + y) * 24, 8), 24), :
        ]

    k_part[:B, :B] = 0.5 * (k_part[:B, :B] + k_part[:B, :B].T)

    @pl.loop(0, 2)
    def _(c):
        cols, right = columns(c), columns(c + 2)
        z1e = mm(split(k_part[:B, :B]), (th[0, 0, :, cols], th[1, 0, :, cols]))
        k12 = k_part[:B, right]
        xt[:B, right] = z1e - k12
        turned = mm((th[0, 1], th[1, 1]), split(k12 - 0.5 * z1e))
        k_part[B:, cols] = 0.5 * k_part[B:, cols] - turned[:256]
        k_part[B:, right] = 0.5 * k_part[B:, right] - turned[256:]

    xt[:B, :B] = -k_part[:B, :B]
    for c, ref, rows in ((0, xt, slice(B, M)), (1, e_part, slice(0, 256))):
        cols, right = slice(256 * c, 256 * c + 256), slice(B + 256 * c, B + 256 * c + 256)
        ref[rows, :B] = xt[:B, right].T
        turned = jnp.concatenate([k_part[B:, cols].T, k_part[B:, right].T], axis=1)
        ref[rows, B:] = -(k_part[B:, B * c : B * c + B] + turned)
    for i in range(4):
        rows = xt[256 * i : 256 * i + 256, :] if i < 3 else e_part[...]
        put(p2, (slice(256 * i, 256 * i + 256), EVERY), mm(split(rows), hl(uch, EVERY, EVERY), NT))

    def add_to_tile(j, scale, value):
        for slot in range(16):
            tile_row = slot // 4 % 2 * 8 + slot % 4 * 2 + slot // 8
            for e in range(2):
                where = pl.ds(tile_row * (6 * W) + j * 2 + e, W, stride=6)
                hb[where, :] = scale * hb[where, :] - value[slot * W : (slot + 1) * W, 128 * e : 128 * e + 128]

    @pl.loop(0, 3)
    def _(j):
        add_to_tile(j, 0.5, mm(hl(urh, EVERY, EVERY), hl(p2, EVERY, columns(j))))

    next(col_steps)
    next(row_steps)

    @pl.loop(0, 3)
    def _(i):
        put(p0, (columns(i), EVERY), xr[columns(i), :])
        put(p1, (columns(i), EVERY), xc[columns(i), :])

    @pl.loop(0, 3)
    def _(j):
        rows = columns(j)
        value = mm(hl(p0, EVERY, ONE), hl(bch, rows, EVERY), NT)
        value = value + mm(hl(p0, EVERY, TWO), hl(uch, rows, TWO), NT)
        value = value + mm(hl(brh, EVERY, EVERY), hl(p1, rows, ONE), NT)
        value = value + mm(hl(urh, EVERY, TWO), hl(p1, rows, TWO), NT)
        add_to_tile(j, 1.0, value)

    for copy in m_copies:
        copy.wait_recv()

    @pl.loop(0, 16)
    def _(slot):
        tile_row = slot // 4 % 2 * 8 + slot % 4 * 2 + slot // 8
        for j in range(6):
            where = pl.ds(tile_row * (6 * W) + j, W, stride=6)
            hb[where, :] = hb[where, :] + 0.5 * m[j // 3, rows48(slot), 128 * (j % 3) : 128 * (j % 3) + 128]

    mail.settle()
    last = pltpu.make_async_copy(hb, out, local_sems.at[3])
    last.start()
    last.wait()


def vmem(*shape, dtype=F32):
    return pltpu.VMEM(shape, dtype)


def on_device(hessian, panels, factors):
    anywhere = pl.BlockSpec(memory_space=pl.ANY)

    def sums(rows):
        return [vmem(rows, U), vmem(rows, U), vmem(rows // 2, U), vmem(rows * 3 // 8, U),
                vmem(rows * 3 // 32, U), vmem(rows * 7 // 32, 128)]

    updated = pl.pallas_call(
        kernel,
        name="panels",
        out_shape=jax.ShapeDtypeStruct((M * 6, 128), F32),
        in_specs=[anywhere, pl.BlockSpec(memory_space=pltpu.VMEM), anywhere],
        out_specs=anywhere,
        scratch_shapes=[
            vmem(M * 6, 128), vmem(2, M, 384), vmem(8, 192, 384), vmem(4, 8, W, 384), vmem(2, M, 384),
            vmem(M, U), vmem(M, U), vmem(2, 2, B, B, dtype=BF16),
            *[vmem(2, M, U, dtype=BF16)] * 4, vmem(2, U, M, dtype=BF16), *[vmem(2, M, B, dtype=BF16)] * 2,
            *sums(256),
            vmem(M, U), vmem(2, 4, W, B), vmem(2, 4, W, U), vmem(3, W, U), vmem(M // 2, U), vmem(3, 2, W, U), vmem(W, U),
            *sums(M),
            pltpu.SemaphoreType.DMA((184,)), pltpu.SemaphoreType.DMA((184,)), pltpu.SemaphoreType.DMA((4,)),
        ],
        compiler_params=pltpu.CompilerParams(
            collective_id=0, has_side_effects=True, vmem_limit_bytes=63 << 20
        ),
    )(hessian.reshape(M * 6, 128), panels.reshape(W, U), factors)
    return updated.reshape(1, M, 1, M)


def solution(mesh):
    return jax.shard_map(
        on_device,
        mesh=mesh,
        in_specs=(P("row", None, "col", None), P("row", "col", None, None), P()),
        out_specs=P("row", None, "col", None),
        check_vma=False,
    )
```

```python
import jax
import jax.numpy as jnp
from jax import lax
from jax.experimental import pallas as pl
from jax.experimental.pallas import tpu as pltpu
from jax.sharding import PartitionSpec as P

MESH = pl.DeviceIdType.MESH
F32, BF16 = jnp.float32, jnp.bfloat16
NX, NY, NZ = 4, 4, 8
W = 48
M = 768
B = 512
U = 2 * B


def split(value):
    high = value.astype(BF16)
    return high, (value - high.astype(F32)).astype(BF16)


def put(ref, where, value):
    high, low = split(value)
    ref[(0,) + where] = high
    ref[(1,) + where] = low


def mm(left, right, dims=((1,), (0,))):
    def one(a, b):
        return lax.dot_general(a, b, (dims, ((), ())), preferred_element_type=F32)

    return one(left[0], right[0]) + (one(left[0], right[1]) + one(left[1], right[0]))


NT = ((1,), (1,))


def hl(ref, *where):
    return ref[(0,) + where], ref[(1,) + where]


class Place:
    def __init__(self):
        row, col = lax.axis_index("row"), lax.axis_index("col")
        self.zh, self.x = row // NX, row % NX
        self.zl, self.y, self.k = col // (2 * NY), (col // 2) % NY, col % 2
        self.z = self.zh * 2 + self.zl
        self.f = row
        self.slot = self.slot_of(self.k, self.zl, self.y)

    def slot_of(self, k, zl, y):
        return k * 8 + zl * 4 + y

    def at(self, dx=0, dy=0, dz=0, dk=0):
        x, y, z = (self.x + dx) % NX, (self.y + dy) % NY, (self.z + dz) % NZ
        k = (self.k + dk) % 2
        return {"row": (z // 2) * NX + x, "col": (z % 2) * 2 * NY + y * 2 + k}

    def zl_peer(self):
        return {"col": (1 - self.zl) * 2 * NY + self.y * 2 + self.k, "row": self.f}


class Mail:
    def __init__(self, send_sems, recv_sems):
        self.send_sems, self.recv_sems, self.open, self.count = send_sems, recv_sems, [], 0

    def send(self, src, dst, target):
        index = self.count
        self.count += 1
        copy = pltpu.make_async_remote_copy(
            src, dst, self.send_sems.at[index], self.recv_sems.at[index], device_id=target, device_id_type=MESH
        )
        copy.start()
        self.open.append(copy)
        return copy

    def settle(self, copies=None):
        leaving = list(self.open if copies is None else copies)
        for copy in leaving:
            copy.wait_send()
        self.open = [copy for copy in self.open if not any(copy is other for other in leaving)]


def greet(partners):
    barrier = pltpu.get_barrier_semaphore()
    for target in partners:
        pl.semaphore_signal(barrier, inc=1, device_id=target, device_id_type=MESH)
    pl.semaphore_wait(barrier, len(partners))


def rows48(slot):
    return pl.ds(pl.multiple_of(slot * W, 8), W)


def logged(mail, log):
    def send(*args):
        log.append(mail.send(*args))
        return log[-1]

    return send


def gather_row(mail, here, buf, log):
    send = logged(mail, log)
    halves = []

    def block(zh, x):
        return buf.at[rows48(zh % 4 * NX + x % NX)]

    def half(zh, x, which):
        return buf.at[rows48(zh % 4 * NX + x % NX), pl.ds(which * B, B)]

    def both(zh):
        mine = block(zh, here.x)
        return zh, send(mine, mine, here.at(dx=1)), send(mine, mine, here.at(dx=3))

    def pass_on(zh, from_left, from_right):
        from_left.wait_recv()
        part = half(zh, here.x + 3, 0)
        halves.append(send(part, part, here.at(dx=1)))
        from_right.wait_recv()
        part = half(zh, here.x + 1, 1)
        halves.append(send(part, part, here.at(dx=3)))

    mine = block(here.zh, here.x)
    far = {d: send(mine, mine, here.at(dz=2 * d)) for d in (1, 3)}
    group = both(here.zh)
    yield
    for d in (1, 3, 2):
        far[d].wait_recv()
        if d == 1:
            far[2] = send(mine, mine, here.at(dz=4))
        later = both(here.zh + 4 - d)
        pass_on(*group)
        group = later
        yield
    pass_on(*group)
    yield
    for copy in halves:
        copy.wait_recv()
    yield


def gather_col(mail, here, buf, log):
    send = logged(mail, log)

    def block(zl, y):
        return buf.at[rows48(here.slot_of(here.k, zl, y % NY))]

    def half(zl, y, which):
        return buf.at[rows48(here.slot_of(here.k, zl, y % NY)), pl.ds(which * B, B)]

    def both(zl):
        mine = block(zl, here.y)
        return zl, send(mine, mine, here.at(dy=1)), send(mine, mine, here.at(dy=3))

    def pass_on(zl, from_left, from_right):
        from_left.wait_recv()
        part = half(zl, here.y + 3, 0)
        one = send(part, part, here.at(dy=1))
        from_right.wait_recv()
        part = half(zl, here.y + 1, 1)
        return zl, one, send(part, part, here.at(dy=3))

    def across(zl, one, two):
        one.wait_recv()
        two.wait_recv()
        part = buf.at[pl.ds(pl.multiple_of((here.k * 8 + zl * 4) * W, 8), 4 * W)]
        return send(part, part, here.at(dk=1))

    mine = block(here.zl, here.y)
    pair = send(mine, mine, here.zl_peer())
    first = both(here.zl)
    yield
    pair.wait_recv()
    second = both(1 - here.zl)
    first = pass_on(*first)
    yield
    second = pass_on(*second)
    first = across(*first)
    yield
    second = across(*second)
    yield
    first.wait_recv()
    second.wait_recv()
    yield


def all_reduce(mail, here, part, out, from_k, from_y, from_x, from_z):
    half = part.shape[0] // 2
    plane, block = half // 4, half // 16

    def rows(start, count):
        return pl.ds(pl.multiple_of(start, 8), count)

    def lanes(z):
        return pl.ds(pl.multiple_of(z * 128, 128), 128)

    def add(where, ref, count):
        total = part[where, :]
        for p in range(3):
            total = total + ref[p * count : (p + 1) * count, :]
        part[where, :] = total

    copy = mail.send(part.at[rows((1 - here.k) * half, half)], from_k, here.at(dk=1))
    yield
    copy.wait_recv()
    base = here.k * half

    @pl.loop(0, 4)
    def _(i):
        where = rows(base + i * plane, plane)
        part[where, :] = part[where, :] + from_k[rows(i * plane, plane), :]

    copies = [
        mail.send(
            part.at[rows(base + (here.y + d) % 4 * plane, plane)],
            from_y.at[pl.ds((d - 1) * plane, plane)],
            here.at(dy=d),
        )
        for d in (1, 2, 3)
    ]
    yield
    for copy in copies:
        copy.wait_recv()
    base = base + here.y * plane
    add(rows(base, plane), from_y, plane)
    copies = [
        mail.send(
            part.at[rows(base + (here.x + d) % 4 * block, block)],
            from_x.at[pl.ds((d - 1) * block, block)],
            here.at(dx=d),
        )
        for d in (1, 2, 3)
    ]
    yield
    for copy in copies:
        copy.wait_recv()
    where = rows(base + here.x * block, block)
    add(where, from_x, block)
    copies = [
        mail.send(
            part.at[where, lanes((here.z + d) % 8)], from_z.at[pl.ds((d - 1) * block, block)], here.at(dz=d)
        )
        for d in range(1, 8)
    ]
    yield
    for copy in copies:
        copy.wait_recv()
    total = part[where, lanes(here.z)]
    for p in range(7):
        total = total + from_z[p * block : (p + 1) * block, :]
    base = (here.k * 4 + here.y) * plane
    where = rows(base + here.x * block, block)
    out[where, lanes(here.z)] = total
    mine = out.at[where, lanes(here.z)]
    copies = [mail.send(mine, mine, here.at(dz=d)) for d in range(1, 8)]
    yield
    for copy in copies:
        copy.wait_recv()
    mine = out.at[where]
    copies = [mail.send(mine, mine, here.at(dx=d)) for d in (1, 2, 3)]
    yield
    for copy in copies:
        copy.wait_recv()
    mine = out.at[rows(base, plane)]
    copies = [mail.send(mine, mine, here.at(dy=d)) for d in (1, 2, 3)]
    yield
    for copy in copies:
        copy.wait_recv()
    mine = out.at[rows(here.k * half, half)]
    copy = mail.send(mine, mine, here.at(dk=1))
    yield
    copy.wait_recv()
    yield


def columns(j):
    return pl.ds(pl.multiple_of(j * 256, 256), 256)


EVERY, ONE, TWO = slice(None), slice(0, B), slice(B, U)


def kernel(
    h, u, t, out,
    hb, lt, bz, bx, m, uc, ur, th,
    uch, urh, p0, p1, p2, bch, brh,
    e_part, e_out, e_k, e_y, e_x, e_z,
    xt, q0, q1, q2, r1, r2, r3,
    k_part, k_out, k_k, k_y, k_x, k_z,
    send_sems, recv_sems, local_sems,
):
    here = Place()
    loads = [
        pltpu.make_async_copy(t.at[0], xt.at[pl.ds(0, B), pl.ds(0, B)], local_sems.at[0]),
        pltpu.make_async_copy(t.at[1], xt.at[pl.ds(0, B), pl.ds(B, B)], local_sems.at[1]),
        pltpu.make_async_copy(h, hb, local_sems.at[2]),
    ]
    for copy in loads:
        copy.start()
    greet(
        [here.at(dx=d) for d in (1, 2, 3)]
        + [here.at(dz=d) for d in range(1, 8)]
        + [here.at(dy=d, dk=e) for d in range(4) for e in range(2) if d or e]
    )
    mail = Mail(send_sems, recv_sems)
    uc[rows48(here.f), :] = u[...]
    ur[rows48(here.slot), :] = u[...]
    row_log, col_log = [], []
    row_steps, col_steps = gather_row(mail, here, uc, row_log), gather_col(mail, here, ur, col_log)
    next(row_steps)
    next(col_steps)

    loads[0].wait()
    loads[1].wait()
    for p in range(2):
        high, low = split(xt[:B, p * B : p * B + B])
        th[0, p], th[1, p] = high, low
    own_second = split(mm(split(u[:, B:]), (th[0, 1], th[1, 1])))
    part = mm(split(u[:, :B].T), own_second)
    e_part[:, :B] = part[:256]
    e_part[:, B:] = part[256:]
    e_steps = all_reduce(mail, here, e_part, e_out, e_k, e_y, e_x, e_z)
    next(e_steps)
    next(col_steps)

    loads[2].wait()
    for zl in range(2):
        for j in range(6):
            pieces = [
                hb[pl.ds((zl * 8 + y * 2 + k) * 6 * W + j, W, stride=6), :] for k in range(2) for y in range(4)
            ]
            lt[zl, 128 * j : 128 * j + 128, :] = jnp.concatenate(pieces, axis=0).T
    next(row_steps)
    next(row_steps)
    next(row_steps)
    z_copies = {}
    for d in (2, 6, 4, 1, 7, 3, 5):
        z = (here.z + d) % 8
        block = lt.at[z % 2, pl.ds(pl.multiple_of(z // 2 * 192, 8), 192)]
        z_copies[d] = mail.send(block, bz.at[here.z], here.at(dz=d))
    bz[here.z] = lt[here.zl, pl.ds(pl.multiple_of(here.zh * 192, 8), 192), :]
    next(col_steps)
    next(row_steps)
    next(col_steps)
    next(e_steps)
    next(col_steps)

    def bases(src, uh, turned):
        @pl.loop(0, 3)
        def _(i):
            rows = columns(i)
            for p in range(2):
                half = split(src[rows, p * B : p * B + B])
                uh[0, rows, p * B : p * B + B] = half[0]
                uh[1, rows, p * B : p * B + B] = half[1]
                turned(rows, p, mm(half, (th[0, p], th[1, p])))

    def row_side(rows, p, value):
        put(p0, (rows, slice(p * B, p * B + B)), value)
        put(p2, (slice(p * B, p * B + B), rows), value.T)

    def col_side(rows, p, value):
        put(p1, (rows, slice(p * B, p * B + B)), value)

    bases(ur, urh, row_side)

    @pl.loop(0, 2)
    def _(i):
        rows = pl.ds(pl.multiple_of(i * 384, 128), 384)
        pieces = [lt[zl, rows, k * 192 : k * 192 + 192] for k in range(2) for zl in range(2)]
        put(p1, (slice(0, 384), slice(0, M)), jnp.concatenate(pieces, axis=1))

        @pl.loop(0, 4)
        def _(j):
            xt[rows, columns(j)] = mm(hl(p1, slice(0, 384), slice(0, M)), hl(p0, EVERY, columns(j)))

    mail.settle(col_log)

    def target(zh, dx):
        return rows48(zh * 4 + (here.x + dx) % 4)

    t_half = []
    for zh in range(4):
        t_half.append(mail.send(xt.at[target(zh, 2), pl.ds(0, B)], q0.at[0, zh], here.at(dx=1)))
        t_half.append(mail.send(xt.at[target(zh, 2), pl.ds(B, B)], q0.at[1, zh], here.at(dx=3)))
    next(row_steps)
    bases(uc, uch, col_side)
    mail.settle(row_log)
    for copy in t_half:
        copy.wait_recv()
    t_x = []
    for zh in range(4):
        xt[target(zh, 1), ONE] = xt[target(zh, 1), ONE] + q0[0, zh]
        xt[target(zh, 3), TWO] = xt[target(zh, 3), TWO] + q0[1, zh]
        t_x.append(mail.send(xt.at[target(zh, 1)], q1.at[0, zh], here.at(dx=1)))
        t_x.append(mail.send(xt.at[target(zh, 3)], q1.at[1, zh], here.at(dx=3)))

    def image(k):
        rows = pl.ds(pl.multiple_of(k * 384, 128), 384)
        for zl in range(2):
            for y in range(4):
                for j in range(6):
                    start = (zl * 8 + y * 2 + k) * 6 * W + j
                    at = (zl * 4 + y) * W
                    put(p0, (slice(at, at + W), slice(128 * j, 128 * j + 128)), hb[pl.ds(start, W, stride=6), :])

        @pl.loop(0, 4)
        def _(j):
            uc[rows, columns(j)] = mm(hl(p0, slice(0, 384), slice(0, M)), hl(p1, EVERY, columns(j)))

        return uc.at[rows]

    x_core = mail.send(image(1 - here.k), r1, here.at(dk=1))
    image(here.k)

    for j in range(4):
        right = split(uc[:, 256 * j : 256 * j + 256])
        c = j % 2
        where = slice(B + 256 * c, B + 256 * c + 256)
        value = mm(hl(p2, ONE, EVERY), right)
        if j < 2:
            k_part[:B, 256 * c : 256 * c + 256] = value
        else:
            k_part[:B, where] = k_part[:B, where] + 0.5 * value
        value = mm(hl(p2, TWO, EVERY), right)
        if j < 2:
            k_part[256 * c : 256 * c + 256, B:] = 0.5 * value.T
        else:
            k_part[B:, 256 * c : 256 * c + 256] = value[:256]
            k_part[B:, where] = value[256:]
    mail.settle([x_core])
    k_steps = all_reduce(mail, here, k_part, k_out, k_k, k_y, k_x, k_z)
    next(k_steps)
    x_core.wait_recv()

    @pl.loop(0, 8)
    def _(i):
        r1[rows48(i), :] = r1[rows48(i), :] + uc[rows48(here.k * 8 + i), :]

    x_y = []
    for d in (1, 2, 3):
        for zl in range(2):
            x_y.append(
                mail.send(r1.at[rows48(zl * 4 + (here.y + d) % 4)], r2.at[d - 1, zl], here.at(dy=d))
            )
    next(k_steps)
    next(e_steps)

    x_copies = {}

    def along_x(d):
        z = (here.z + 8 - d) % 8
        x_copies[d] = []
        for e in (1, 2, 3):
            x_copies[d].append(
                mail.send(bz.at[z, rows48((here.x + e) % 4)], bx.at[here.x, z], here.at(dx=e))
            )
        bx[here.x, z] = bz[z, rows48(here.x), :]

    def shuffle(zl):
        for i in range(8):
            for half in range(2):
                pieces = [
                    bx[x, (half * 2 + zh) * 2 + zl, :, i * W : (i + 1) * W] for zh in range(2) for x in range(4)
                ]
                lt[half, rows48(zl * 8 + i), :] = jnp.concatenate(pieces, axis=1)
        copies = []
        where = rows48(here.slot_of(here.k, zl, here.y))
        for dk in range(2):
            for dy in range(4):
                rows = rows48(zl * 8 + (here.k + dk) % 2 * 4 + (here.y + dy) % 4)
                if dk or dy:
                    copies.append(mail.send(lt.at[:, rows], m.at[:, where], here.at(dy=dy, dk=dk)))
                else:
                    m[:, where, :] = lt[:, rows, :]
        return copies

    for copy in t_x:
        copy.wait_recv()
    for zh in range(4):
        where = target(zh, 0)
        xt[where, :] = xt[where, :] + (q1[0, zh] + q1[1, zh])
    t_z = [
        mail.send(xt.at[rows48((here.zh + d) % 4 * 4 + here.x)], q2.at[d - 1], here.at(dz=2 * d))
        for d in (1, 2, 3)
    ]
    for copy in x_y:
        copy.wait_recv()
    for zl in range(2):
        where = rows48(zl * 4 + here.y)
        r1[where, :] = r1[where, :] + (r2[0, zl] + r2[1, zl] + r2[2, zl])
    x_z = mail.send(r1.at[rows48((1 - here.zl) * 4 + here.y)], r3, here.zl_peer())
    along_x(0)
    for d in (2, 6, 4, 1, 7, 3, 5):
        z_copies[d].wait_recv()
        along_x(d)
    next(e_steps)
    next(k_steps)
    mail.settle(z_copies.values())
    next(k_steps)
    next(e_steps)
    x_z.wait_recv()
    for copy in t_z:
        copy.wait_recv()
    piece = r1[rows48(here.zl * 4 + here.y), :] + r3[...]
    piece = 0.5 * (piece + xt[rows48(here.f), :] + (q2[0] + q2[1] + q2[2]))
    xr, xc = uc, ur
    xc[rows48(here.f), :] = piece
    xr[rows48(here.slot), :] = piece
    closing = list(mail.open)
    row_steps, col_steps = gather_row(mail, here, xc, []), gather_col(mail, here, xr, [])
    next(row_steps)
    next(col_steps)
    next(k_steps)
    next(e_steps)
    next(col_steps)
    next(row_steps)
    next(k_steps)
    next(e_steps)
    next(row_steps)
    next(row_steps)
    next(k_steps)
    next(e_steps)
    m_copies = []
    for zl, deltas in ((here.zl, (0, 2, 6, 4)), (1 - here.zl, (1, 7, 3, 5))):
        for d in deltas:
            for copy in x_copies[d]:
                copy.wait_recv()
        m_copies += shuffle(zl)
    next(row_steps)
    next(col_steps)
    next(col_steps)
    next(e_steps)

    e = jnp.concatenate([e_out[:, :B], e_out[:, B:]], axis=0)
    for p, value in ((0, e), (1, e.T)):
        high, low = split(value)
        th[0, p], th[1, p] = high, low

    def less(uh, bh):
        @pl.loop(0, 3)
        def _(i):
            rows = columns(i)
            first = uh[0, rows, ONE].astype(F32) + uh[1, rows, ONE].astype(F32)
            put(bh, (rows, EVERY), first - mm(hl(uh, rows, TWO), (th[0, 0], th[1, 0]), NT))

    less(uch, bch)
    less(urh, brh)

    def add_to_tile(j, scale, value):
        for slot in range(16):
            tile_row = slot // 4 % 2 * 8 + slot % 4 * 2 + slot // 8
            for e in range(2):
                where = pl.ds(tile_row * (6 * W) + j * 2 + e, W, stride=6)
                hb[where, :] = scale * hb[where, :] - value[slot * W : (slot + 1) * W, 128 * e : 128 * e + 128]

    next(col_steps)
    next(row_steps)

    @pl.loop(0, 3)
    def _(i):
        put(p0, (columns(i), EVERY), xr[columns(i), :])
        put(p1, (columns(i), EVERY), xc[columns(i), :])

    next(k_steps)

    @pl.loop(0, 3)
    def _(j):
        rows = columns(j)
        value = mm(hl(p0, EVERY, ONE), hl(bch, rows, EVERY), NT)
        value = value + mm(hl(p0, EVERY, TWO), hl(uch, rows, TWO), NT)
        value = value + mm(hl(brh, EVERY, EVERY), hl(p1, rows, ONE), NT)
        value = value + mm(hl(urh, EVERY, TWO), hl(p1, rows, TWO), NT)
        add_to_tile(j, 0.5, value)

    next(k_steps)
    mail.settle(closing)

    @pl.loop(0, 3)
    def _(i):
        k_part[columns(i), :] = k_out[columns(i), :]

    k_part[:B, :B] = 0.5 * (k_part[:B, :B] + k_part[:B, :B].T)

    @pl.loop(0, 2)
    def _(c):
        cols, right = columns(c), columns(c + 2)
        z1e = mm(split(k_part[:B, :B]), (th[0, 0, :, cols], th[1, 0, :, cols]))
        k12 = k_part[:B, right]
        xt[:B, right] = z1e - k12
        turned = mm((th[0, 1], th[1, 1]), split(k12 - 0.5 * z1e))
        k_part[B:, cols] = 0.5 * k_part[B:, cols] - turned[:256]
        k_part[B:, right] = 0.5 * k_part[B:, right] - turned[256:]

    xt[:B, :B] = -k_part[:B, :B]
    for c, ref, rows in ((0, xt, slice(B, M)), (1, e_part, slice(0, 256))):
        cols, right = slice(256 * c, 256 * c + 256), slice(B + 256 * c, B + 256 * c + 256)
        ref[rows, :B] = xt[:B, right].T
        turned = jnp.concatenate([k_part[B:, cols].T, k_part[B:, right].T], axis=1)
        ref[rows, B:] = -(k_part[B:, B * c : B * c + B] + turned)
    for i in range(4):
        rows = xt[256 * i : 256 * i + 256, :] if i < 3 else e_part[...]
        put(p2, (slice(256 * i, 256 * i + 256), EVERY), mm(split(rows), hl(uch, EVERY, EVERY), NT))

    @pl.loop(0, 3)
    def _(j):
        add_to_tile(j, 1.0, mm(hl(urh, EVERY, EVERY), hl(p2, EVERY, columns(j))))

    for copy in m_copies:
        copy.wait_recv()

    @pl.loop(0, 16)
    def _(slot):
        tile_row = slot // 4 % 2 * 8 + slot % 4 * 2 + slot // 8
        for j in range(6):
            where = pl.ds(tile_row * (6 * W) + j, W, stride=6)
            hb[where, :] = hb[where, :] + 0.5 * m[j // 3, rows48(slot), 128 * (j % 3) : 128 * (j % 3) + 128]

    mail.settle()
    last = pltpu.make_async_copy(hb, out, local_sems.at[3])
    last.start()
    last.wait()


def vmem(*shape, dtype=F32):
    return pltpu.VMEM(shape, dtype)


def on_device(hessian, panels, factors):
    anywhere = pl.BlockSpec(memory_space=pl.ANY)

    def sums(rows):
        return [vmem(rows, U), vmem(rows, U), vmem(rows // 2, U), vmem(rows * 3 // 8, U),
                vmem(rows * 3 // 32, U), vmem(rows * 7 // 32, 128)]

    updated = pl.pallas_call(
        kernel,
        name="panels",
        out_shape=jax.ShapeDtypeStruct((M * 6, 128), F32),
        in_specs=[anywhere, pl.BlockSpec(memory_space=pltpu.VMEM), anywhere],
        out_specs=anywhere,
        scratch_shapes=[
            vmem(M * 6, 128), vmem(2, M, 384), vmem(8, 192, 384), vmem(4, 8, W, 384), vmem(2, M, 384),
            vmem(M, U), vmem(M, U), vmem(2, 2, B, B, dtype=BF16),
            *[vmem(2, M, U, dtype=BF16)] * 4, vmem(2, U, M, dtype=BF16), *[vmem(2, M, B, dtype=BF16)] * 2,
            *sums(256),
            vmem(M, U), vmem(2, 4, W, B), vmem(2, 4, W, U), vmem(3, W, U), vmem(M // 2, U), vmem(3, 2, W, U), vmem(W, U),
            *sums(M),
            pltpu.SemaphoreType.DMA((192,)), pltpu.SemaphoreType.DMA((192,)), pltpu.SemaphoreType.DMA((4,)),
        ],
        compiler_params=pltpu.CompilerParams(
            collective_id=0, has_side_effects=True, vmem_limit_bytes=63 << 20
        ),
    )(hessian.reshape(M * 6, 128), panels.reshape(W, U), factors)
    return updated.reshape(1, M, 1, M)


def solution(mesh):
    return jax.shard_map(
        on_device,
        mesh=mesh,
        in_specs=(P("row", None, "col", None), P("row", "col", None, None), P()),
        out_specs=P("row", None, "col", None),
        check_vma=False,
    )
```

```python
import jax
import jax.numpy as jnp
from jax import lax
from jax.experimental import pallas as pl
from jax.experimental.pallas import tpu as pltpu
from jax.sharding import PartitionSpec as P

MESH = pl.DeviceIdType.MESH
F32, BF16 = jnp.float32, jnp.bfloat16
NX, NY, NZ = 4, 4, 8
W = 48
M = 768
B = 512
U = 2 * B


def split(value):
    high = value.astype(BF16)
    return high, (value - high.astype(F32)).astype(BF16)


def put(ref, where, value):
    high, low = split(value)
    ref[(0,) + where] = high
    ref[(1,) + where] = low


def mm(left, right, dims=((1,), (0,))):
    def one(a, b):
        return lax.dot_general(a, b, (dims, ((), ())), preferred_element_type=F32)

    return one(left[0], right[0]) + (one(left[0], right[1]) + one(left[1], right[0]))


NT = ((1,), (1,))


def hl(ref, *where):
    return ref[(0,) + where], ref[(1,) + where]


class Place:
    def __init__(self):
        row, col = lax.axis_index("row"), lax.axis_index("col")
        self.zh, self.x = row // NX, row % NX
        self.zl, self.y, self.k = col // (2 * NY), (col // 2) % NY, col % 2
        self.z = self.zh * 2 + self.zl
        self.f = row
        self.slot = self.slot_of(self.k, self.zl, self.y)

    def slot_of(self, k, zl, y):
        return k * 8 + zl * 4 + y

    def at(self, dx=0, dy=0, dz=0, dk=0):
        x, y, z = (self.x + dx) % NX, (self.y + dy) % NY, (self.z + dz) % NZ
        k = (self.k + dk) % 2
        return {"row": (z // 2) * NX + x, "col": (z % 2) * 2 * NY + y * 2 + k}

    def zl_peer(self):
        return {"col": (1 - self.zl) * 2 * NY + self.y * 2 + self.k, "row": self.f}


class Mail:
    def __init__(self, send_sems, recv_sems):
        self.send_sems, self.recv_sems, self.open, self.count = send_sems, recv_sems, [], 0

    def send(self, src, dst, target):
        index = self.count
        self.count += 1
        copy = pltpu.make_async_remote_copy(
            src, dst, self.send_sems.at[index], self.recv_sems.at[index], device_id=target, device_id_type=MESH
        )
        copy.start()
        self.open.append(copy)
        return copy

    def settle(self, copies=None):
        leaving = list(self.open if copies is None else copies)
        for copy in leaving:
            copy.wait_send()
        self.open = [copy for copy in self.open if not any(copy is other for other in leaving)]


def greet(partners):
    barrier = pltpu.get_barrier_semaphore()
    for target in partners:
        pl.semaphore_signal(barrier, inc=1, device_id=target, device_id_type=MESH)
    pl.semaphore_wait(barrier, len(partners))


def rows48(slot):
    return pl.ds(pl.multiple_of(slot * W, 8), W)


def logged(mail, log):
    def send(*args):
        log.append(mail.send(*args))
        return log[-1]

    return send


def gather_row(mail, here, buf, log):
    send = logged(mail, log)
    halves = []

    def block(zh, x):
        return buf.at[rows48(zh % 4 * NX + x % NX)]

    def half(zh, x, which):
        return buf.at[rows48(zh % 4 * NX + x % NX), pl.ds(which * B, B)]

    def both(zh):
        mine = block(zh, here.x)
        return zh, send(mine, mine, here.at(dx=1)), send(mine, mine, here.at(dx=3))

    def pass_on(zh, from_left, from_right):
        from_left.wait_recv()
        part = half(zh, here.x + 3, 0)
        halves.append(send(part, part, here.at(dx=1)))
        from_right.wait_recv()
        part = half(zh, here.x + 1, 1)
        halves.append(send(part, part, here.at(dx=3)))

    mine = block(here.zh, here.x)
    far = {d: send(mine, mine, here.at(dz=2 * d)) for d in (1, 3)}
    group = both(here.zh)
    yield
    for d in (1, 3, 2):
        far[d].wait_recv()
        if d == 1:
            far[2] = send(mine, mine, here.at(dz=4))
        later = both(here.zh + 4 - d)
        pass_on(*group)
        group = later
        yield
    pass_on(*group)
    yield
    for copy in halves:
        copy.wait_recv()
    yield


def gather_col(mail, here, buf, log):
    send = logged(mail, log)

    def block(zl):
        return buf.at[rows48(here.slot_of(here.k, zl, here.y))]

    mine = block(here.zl)
    pair = send(mine, mine, here.zl_peer())
    first = [send(mine, mine, here.at(dy=d)) for d in (1, 2, 3)]
    yield
    pair.wait_recv()
    got = block(1 - here.zl)
    second = [send(got, got, here.at(dy=d)) for d in (1, 2, 3)]
    yield
    last = []
    for zl, copies in ((here.zl, first), (1 - here.zl, second)):
        for copy in copies:
            copy.wait_recv()
        part = buf.at[pl.ds(pl.multiple_of((here.k * 8 + zl * 4) * W, 8), 4 * W)]
        last.append(send(part, part, here.at(dk=1)))
        yield
    for copy in last:
        copy.wait_recv()
    yield


def all_reduce(mail, here, part, out, from_k, from_y, from_x, from_z, swap):
    half = part.shape[0] // 2
    plane, block = half // 4, half // 16

    def rows(start, count):
        return pl.ds(pl.multiple_of(start, 8), count)

    def lanes(z):
        return pl.ds(pl.multiple_of(z * 128, 128), 128)

    def add(where, ref, count):
        total = part[where, :]
        for p in range(3):
            total = total + ref[p * count : (p + 1) * count, :]
        part[where, :] = total

    copy = mail.send(part.at[rows((1 - here.k) * half, half)], from_k, here.at(dk=1))
    yield
    copy.wait_recv()
    base = here.k * half

    @pl.loop(0, 4)
    def _(i):
        where = rows(base + i * plane, plane)
        part[where, :] = part[where, :] + from_k[rows(i * plane, plane), :]

    copies = [
        mail.send(
            part.at[rows(base + (here.y + d) % 4 * plane, plane)],
            from_y.at[pl.ds((d - 1) * plane, plane)],
            here.at(dy=d),
        )
        for d in (1, 2, 3)
    ]
    yield
    for copy in copies:
        copy.wait_recv()
    base = base + here.y * plane
    add(rows(base, plane), from_y, plane)
    copies = [
        mail.send(
            part.at[rows(base + (here.x + d) % 4 * block, block)],
            from_x.at[pl.ds((d - 1) * block, block)],
            here.at(dx=d),
        )
        for d in (1, 2, 3)
    ]
    yield
    for copy in copies:
        copy.wait_recv()
    where = rows(base + here.x * block, block)
    add(where, from_x, block)
    copies = [
        mail.send(
            part.at[where, lanes((here.z + d) % 8)], from_z.at[pl.ds((d - 1) * block, block)], here.at(dz=d)
        )
        for d in range(1, 8)
    ]
    yield
    for copy in copies:
        copy.wait_recv()
    total = part[where, lanes(here.z)]
    for p in range(7):
        total = total + from_z[p * block : (p + 1) * block, :]
    outer, inner = (here.x, here.y) if swap else (here.y, here.x)
    base = (here.k * 4 + outer) * plane
    where = rows(base + inner * block, block)
    out[where, lanes(here.z)] = total
    mine = out.at[where, lanes(here.z)]
    copies = [mail.send(mine, mine, here.at(dz=d)) for d in range(1, 8)]
    yield
    for copy in copies:
        copy.wait_recv()
    mine = out.at[where]
    copies = [mail.send(mine, mine, here.at(dy=d) if swap else here.at(dx=d)) for d in (1, 2, 3)]
    yield
    for copy in copies:
        copy.wait_recv()
    mine = out.at[rows(base, plane)]
    copies = [mail.send(mine, mine, here.at(dx=d) if swap else here.at(dy=d)) for d in (1, 2, 3)]
    yield
    for copy in copies:
        copy.wait_recv()
    mine = out.at[rows(here.k * half, half)]
    copy = mail.send(mine, mine, here.at(dk=1))
    yield
    copy.wait_recv()
    yield


def columns(j):
    return pl.ds(pl.multiple_of(j * 256, 256), 256)


EVERY, ONE, TWO = slice(None), slice(0, B), slice(B, U)


def kernel(
    h, u, t, out,
    hb, lt, bz, bx, m, uc, ur, th,
    uch, urh, p0, p1, p2, bch, brh,
    e_part, e_out, e_k, e_y, e_x, e_z,
    xt, q0, q1, q2, r1, r2, r3,
    k_part, k_out, k_k, k_y, k_x, k_z,
    send_sems, recv_sems, local_sems,
):
    here = Place()
    loads = [
        pltpu.make_async_copy(t.at[0], xt.at[pl.ds(0, B), pl.ds(0, B)], local_sems.at[0]),
        pltpu.make_async_copy(t.at[1], xt.at[pl.ds(0, B), pl.ds(B, B)], local_sems.at[1]),
        pltpu.make_async_copy(h, hb, local_sems.at[2]),
    ]
    for copy in loads:
        copy.start()
    greet(
        [here.at(dx=d) for d in (1, 2, 3)]
        + [here.at(dz=d) for d in range(1, 8)]
        + [here.at(dy=d, dk=e) for d in range(4) for e in range(2) if d or e]
    )
    mail = Mail(send_sems, recv_sems)
    uc[rows48(here.f), :] = u[...]
    ur[rows48(here.slot), :] = u[...]
    row_log, col_log = [], []
    row_steps, col_steps = gather_row(mail, here, uc, row_log), gather_col(mail, here, ur, col_log)
    next(row_steps)
    next(col_steps)

    loads[0].wait()
    loads[1].wait()
    for p in range(2):
        high, low = split(xt[:B, p * B : p * B + B])
        th[0, p], th[1, p] = high, low
    own_second = split(mm(split(u[:, B:]), (th[0, 1], th[1, 1])))
    part = mm(split(u[:, :B].T), own_second)
    e_part[:, :B] = part[:256]
    e_part[:, B:] = part[256:]
    e_steps = all_reduce(mail, here, e_part, e_out, e_k, e_y, e_x, e_z, False)
    next(e_steps)
    next(col_steps)

    loads[2].wait()
    for zl in range(2):
        for j in range(6):
            pieces = [
                hb[pl.ds((zl * 8 + y * 2 + k) * 6 * W + j, W, stride=6), :] for k in range(2) for y in range(4)
            ]
            lt[zl, 128 * j : 128 * j + 128, :] = jnp.concatenate(pieces, axis=0).T
    next(row_steps)
    next(row_steps)
    next(row_steps)
    z_copies = {}
    for d in (2, 6, 4, 1, 7, 3, 5):
        z = (here.z + d) % 8
        block = lt.at[z % 2, pl.ds(pl.multiple_of(z // 2 * 192, 8), 192)]
        z_copies[d] = mail.send(block, bz.at[here.z], here.at(dz=d))
    bz[here.z] = lt[here.zl, pl.ds(pl.multiple_of(here.zh * 192, 8), 192), :]
    next(col_steps)
    next(row_steps)
    next(col_steps)
    next(e_steps)
    next(col_steps)

    def bases(src, uh, turned):
        @pl.loop(0, 3)
        def _(i):
            rows = columns(i)
            for p in range(2):
                half = split(src[rows, p * B : p * B + B])
                uh[0, rows, p * B : p * B + B] = half[0]
                uh[1, rows, p * B : p * B + B] = half[1]
                turned(rows, p, mm(half, (th[0, p], th[1, p])))

    def row_side(rows, p, value):
        put(p0, (rows, slice(p * B, p * B + B)), value)
        put(p2, (slice(p * B, p * B + B), rows), value.T)

    def col_side(rows, p, value):
        put(p1, (rows, slice(p * B, p * B + B)), value)

    bases(ur, urh, row_side)

    @pl.loop(0, 2)
    def _(i):
        rows = pl.ds(pl.multiple_of(i * 384, 128), 384)
        pieces = [lt[zl, rows, k * 192 : k * 192 + 192] for k in range(2) for zl in range(2)]
        put(p1, (slice(0, 384), slice(0, M)), jnp.concatenate(pieces, axis=1))

        @pl.loop(0, 4)
        def _(j):
            xt[rows, columns(j)] = mm(hl(p1, slice(0, 384), slice(0, M)), hl(p0, EVERY, columns(j)))

    mail.settle(col_log)

    def target(zh, dx):
        return rows48(zh * 4 + (here.x + dx) % 4)

    t_half = []
    for zh in range(4):
        t_half.append(mail.send(xt.at[target(zh, 2), pl.ds(0, B)], q0.at[0, zh], here.at(dx=1)))
        t_half.append(mail.send(xt.at[target(zh, 2), pl.ds(B, B)], q0.at[1, zh], here.at(dx=3)))
    next(row_steps)
    bases(uc, uch, col_side)
    mail.settle(row_log)
    for copy in t_half:
        copy.wait_recv()
    t_x = []
    for zh in range(4):
        xt[target(zh, 1), ONE] = xt[target(zh, 1), ONE] + q0[0, zh]
        xt[target(zh, 3), TWO] = xt[target(zh, 3), TWO] + q0[1, zh]
        t_x.append(mail.send(xt.at[target(zh, 1)], q1.at[0, zh], here.at(dx=1)))
        t_x.append(mail.send(xt.at[target(zh, 3)], q1.at[1, zh], here.at(dx=3)))

    def image(k):
        rows = pl.ds(pl.multiple_of(k * 384, 128), 384)
        for zl in range(2):
            for y in range(4):
                for j in range(6):
                    start = (zl * 8 + y * 2 + k) * 6 * W + j
                    at = (zl * 4 + y) * W
                    put(p0, (slice(at, at + W), slice(128 * j, 128 * j + 128)), hb[pl.ds(start, W, stride=6), :])

        @pl.loop(0, 4)
        def _(j):
            uc[rows, columns(j)] = mm(hl(p0, slice(0, 384), slice(0, M)), hl(p1, EVERY, columns(j)))

        return uc.at[rows]

    x_core = mail.send(image(1 - here.k), r1, here.at(dk=1))
    image(here.k)

    for j in range(4):
        right = split(uc[:, 256 * j : 256 * j + 256])
        c = j % 2
        where = slice(B + 256 * c, B + 256 * c + 256)
        value = mm(hl(p2, ONE, EVERY), right)
        if j < 2:
            k_part[:B, 256 * c : 256 * c + 256] = value
        else:
            k_part[:B, where] = k_part[:B, where] + 0.5 * value
        value = mm(hl(p2, TWO, EVERY), right)
        if j < 2:
            k_part[256 * c : 256 * c + 256, B:] = 0.5 * value.T
        else:
            k_part[B:, 256 * c : 256 * c + 256] = value[:256]
            k_part[B:, where] = value[256:]
    mail.settle([x_core])
    k_steps = all_reduce(mail, here, k_part, k_out, k_k, k_y, k_x, k_z, True)
    next(k_steps)
    x_core.wait_recv()

    @pl.loop(0, 8)
    def _(i):
        r1[rows48(i), :] = r1[rows48(i), :] + uc[rows48(here.k * 8 + i), :]

    x_y = []
    for d in (1, 2, 3):
        for zl in range(2):
            x_y.append(
                mail.send(r1.at[rows48(zl * 4 + (here.y + d) % 4)], r2.at[d - 1, zl], here.at(dy=d))
            )
    next(k_steps)
    next(e_steps)

    x_copies = {}

    def along_x(d):
        z = (here.z + 8 - d) % 8
        x_copies[d] = []
        for e in (1, 2, 3):
            x_copies[d].append(
                mail.send(bz.at[z, rows48((here.x + e) % 4)], bx.at[here.x, z], here.at(dx=e))
            )
        bx[here.x, z] = bz[z, rows48(here.x), :]

    def shuffle(zl):
        for i in range(8):
            for half in range(2):
                pieces = [
                    bx[x, (half * 2 + zh) * 2 + zl, :, i * W : (i + 1) * W] for zh in range(2) for x in range(4)
                ]
                lt[half, rows48(zl * 8 + i), :] = jnp.concatenate(pieces, axis=1)
        copies = []
        where = rows48(here.slot_of(here.k, zl, here.y))
        for dk in range(2):
            for dy in range(4):
                rows = rows48(zl * 8 + (here.k + dk) % 2 * 4 + (here.y + dy) % 4)
                if dk or dy:
                    copies.append(mail.send(lt.at[:, rows], m.at[:, where], here.at(dy=dy, dk=dk)))
                else:
                    m[:, where, :] = lt[:, rows, :]
        return copies

    for copy in t_x:
        copy.wait_recv()
    for zh in range(4):
        where = target(zh, 0)
        xt[where, :] = xt[where, :] + (q1[0, zh] + q1[1, zh])
    t_z = [
        mail.send(xt.at[rows48((here.zh + d) % 4 * 4 + here.x)], q2.at[d - 1], here.at(dz=2 * d))
        for d in (1, 2, 3)
    ]
    for copy in x_y:
        copy.wait_recv()
    for zl in range(2):
        where = rows48(zl * 4 + here.y)
        r1[where, :] = r1[where, :] + (r2[0, zl] + r2[1, zl] + r2[2, zl])
    x_z = mail.send(r1.at[rows48((1 - here.zl) * 4 + here.y)], r3, here.zl_peer())
    along_x(0)
    for d in (2, 6, 4, 1, 7, 3, 5):
        z_copies[d].wait_recv()
        along_x(d)
    next(e_steps)
    next(k_steps)
    mail.settle(z_copies.values())
    next(k_steps)
    next(e_steps)
    x_z.wait_recv()
    for copy in t_z:
        copy.wait_recv()
    piece = r1[rows48(here.zl * 4 + here.y), :] + r3[...]
    piece = 0.5 * (piece + xt[rows48(here.f), :] + (q2[0] + q2[1] + q2[2]))
    xr, xc = uc, ur
    xc[rows48(here.f), :] = piece
    xr[rows48(here.slot), :] = piece
    closing = list(mail.open)
    row_steps, col_steps = gather_row(mail, here, xc, []), gather_col(mail, here, xr, [])
    next(row_steps)
    next(col_steps)
    next(k_steps)
    next(e_steps)
    next(col_steps)
    next(row_steps)
    next(k_steps)
    next(e_steps)
    next(row_steps)
    next(row_steps)
    next(k_steps)
    next(e_steps)
    m_copies = []
    for zl, deltas in ((here.zl, (0, 2, 6, 4)), (1 - here.zl, (1, 7, 3, 5))):
        for d in deltas:
            for copy in x_copies[d]:
                copy.wait_recv()
        m_copies += shuffle(zl)
    next(row_steps)
    next(col_steps)
    next(col_steps)
    next(e_steps)

    e = jnp.concatenate([e_out[:, :B], e_out[:, B:]], axis=0)
    for p, value in ((0, e), (1, e.T)):
        high, low = split(value)
        th[0, p], th[1, p] = high, low

    def less(uh, bh):
        @pl.loop(0, 3)
        def _(i):
            rows = columns(i)
            first = uh[0, rows, ONE].astype(F32) + uh[1, rows, ONE].astype(F32)
            put(bh, (rows, EVERY), first - mm(hl(uh, rows, TWO), (th[0, 0], th[1, 0]), NT))

    less(uch, bch)
    less(urh, brh)

    def add_to_tile(j, scale, value):
        for slot in range(16):
            tile_row = slot // 4 % 2 * 8 + slot % 4 * 2 + slot // 8
            for e in range(2):
                where = pl.ds(tile_row * (6 * W) + j * 2 + e, W, stride=6)
                hb[where, :] = scale * hb[where, :] - value[slot * W : (slot + 1) * W, 128 * e : 128 * e + 128]

    next(col_steps)
    next(row_steps)

    @pl.loop(0, 3)
    def _(i):
        put(p0, (columns(i), EVERY), xr[columns(i), :])
        put(p1, (columns(i), EVERY), xc[columns(i), :])

    next(k_steps)

    @pl.loop(0, 3)
    def _(j):
        rows = columns(j)
        value = mm(hl(p0, EVERY, ONE), hl(bch, rows, EVERY), NT)
        value = value + mm(hl(p0, EVERY, TWO), hl(uch, rows, TWO), NT)
        value = value + mm(hl(brh, EVERY, EVERY), hl(p1, rows, ONE), NT)
        value = value + mm(hl(urh, EVERY, TWO), hl(p1, rows, TWO), NT)
        add_to_tile(j, 0.5, value)

    next(k_steps)
    mail.settle(closing)

    @pl.loop(0, 32)
    def _(i):
        k, y, x = i // 16, i // 4 % 4, i % 4
        k_part[pl.ds(pl.multiple_of(i * 24, 8), 24), :] = k_out[
            pl.ds(pl.multiple_of((k * 16 + x * 4 + y) * 24, 8), 24), :
        ]

    k_part[:B, :B] = 0.5 * (k_part[:B, :B] + k_part[:B, :B].T)

    @pl.loop(0, 2)
    def _(c):
        cols, right = columns(c), columns(c + 2)
        z1e = mm(split(k_part[:B, :B]), (th[0, 0, :, cols], th[1, 0, :, cols]))
        k12 = k_part[:B, right]
        xt[:B, right] = z1e - k12
        turned = mm((th[0, 1], th[1, 1]), split(k12 - 0.5 * z1e))
        k_part[B:, cols] = 0.5 * k_part[B:, cols] - turned[:256]
        k_part[B:, right] = 0.5 * k_part[B:, right] - turned[256:]

    xt[:B, :B] = -k_part[:B, :B]
    for c, ref, rows in ((0, xt, slice(B, M)), (1, e_part, slice(0, 256))):
        cols, right = slice(256 * c, 256 * c + 256), slice(B + 256 * c, B + 256 * c + 256)
        ref[rows, :B] = xt[:B, right].T
        turned = jnp.concatenate([k_part[B:, cols].T, k_part[B:, right].T], axis=1)
        ref[rows, B:] = -(k_part[B:, B * c : B * c + B] + turned)
    for i in range(4):
        rows = xt[256 * i : 256 * i + 256, :] if i < 3 else e_part[...]
        put(p2, (slice(256 * i, 256 * i + 256), EVERY), mm(split(rows), hl(uch, EVERY, EVERY), NT))

    @pl.loop(0, 3)
    def _(j):
        add_to_tile(j, 1.0, mm(hl(urh, EVERY, EVERY), hl(p2, EVERY, columns(j))))

    for copy in m_copies:
        copy.wait_recv()

    @pl.loop(0, 16)
    def _(slot):
        tile_row = slot // 4 % 2 * 8 + slot % 4 * 2 + slot // 8
        for j in range(6):
            where = pl.ds(tile_row * (6 * W) + j, W, stride=6)
            hb[where, :] = hb[where, :] + 0.5 * m[j // 3, rows48(slot), 128 * (j % 3) : 128 * (j % 3) + 128]

    mail.settle()
    last = pltpu.make_async_copy(hb, out, local_sems.at[3])
    last.start()
    last.wait()


def vmem(*shape, dtype=F32):
    return pltpu.VMEM(shape, dtype)


def on_device(hessian, panels, factors):
    anywhere = pl.BlockSpec(memory_space=pl.ANY)

    def sums(rows):
        return [vmem(rows, U), vmem(rows, U), vmem(rows // 2, U), vmem(rows * 3 // 8, U),
                vmem(rows * 3 // 32, U), vmem(rows * 7 // 32, 128)]

    updated = pl.pallas_call(
        kernel,
        name="panels",
        out_shape=jax.ShapeDtypeStruct((M * 6, 128), F32),
        in_specs=[anywhere, pl.BlockSpec(memory_space=pltpu.VMEM), anywhere],
        out_specs=anywhere,
        scratch_shapes=[
            vmem(M * 6, 128), vmem(2, M, 384), vmem(8, 192, 384), vmem(4, 8, W, 384), vmem(2, M, 384),
            vmem(M, U), vmem(M, U), vmem(2, 2, B, B, dtype=BF16),
            *[vmem(2, M, U, dtype=BF16)] * 4, vmem(2, U, M, dtype=BF16), *[vmem(2, M, B, dtype=BF16)] * 2,
            *sums(256),
            vmem(M, U), vmem(2, 4, W, B), vmem(2, 4, W, U), vmem(3, W, U), vmem(M // 2, U), vmem(3, 2, W, U), vmem(W, U),
            *sums(M),
            pltpu.SemaphoreType.DMA((184,)), pltpu.SemaphoreType.DMA((184,)), pltpu.SemaphoreType.DMA((4,)),
        ],
        compiler_params=pltpu.CompilerParams(
            collective_id=0, has_side_effects=True, vmem_limit_bytes=63 << 20
        ),
    )(hessian.reshape(M * 6, 128), panels.reshape(W, U), factors)
    return updated.reshape(1, M, 1, M)


def solution(mesh):
    return jax.shard_map(
        on_device,
        mesh=mesh,
        in_specs=(P("row", None, "col", None), P("row", "col", None, None), P()),
        out_specs=P("row", None, "col", None),
        check_vma=False,
    )
```
